32 devices in a mesh: grp: 2 (over y), br: 8 (over z, x), sub: 2 (over core).
Axes of the slice: x: 2, y: 2, z: 4, core: 2. Of those that a mesh axis runs over, the one named last changes fastest.
Arguments:
- charges: bfloat16 [32, 131072], P(None, ('grp', 'br', 'sub')), parts along dimension 1, may hold values from -6 to 6
- order: int32 [131072], P(('grp', 'br', 'sub')), parts along dimension 0, may hold values from 0 to 8191, as said below
- coords: float32 [3, 131072], P(None, ('grp', 'br', 'sub')), parts along dimension 1, may hold values from 0 to 1
- leaf_basis: bfloat16 [1024, 64, 128], P(('grp', 'br', 'sub')), parts along dimension 0, may hold values from -0.5 to 0.5
- leaf_transfer: bfloat16 [1024, 64, 64], P(('grp', 'br', 'sub')), parts along dimension 0, may hold values from -0.375 to 0.375
- branch_transfer: bfloat16 [16, 64, 64], P(('grp', 'br')), parts along dimension 0, may hold values from -0.75 to 0.75
- upper_transfer: bfloat16 [8, 64, 64], P('grp'), parts along dimension 0, may hold values from -0.75 to 0.75
- top_skeleton: float32 [3, 1792], P(None, 'grp'), parts along dimension 1, may hold values from 0 to 1
- near_src: int32 [1024, 27], P(('grp', 'br', 'sub')), parts along dimension 0, may hold values from 0 to 511, as said below
- near_count: int32 [1024], P(('grp', 'br', 'sub')), parts along dimension 0, may hold values from 14 to 27
- far_src: int32 [1024, 6], P(('grp', 'br', 'sub')), parts along dimension 0, may hold values from 0 to 511, as said below
- far_count: int32 [1024], P(('grp', 'br', 'sub')), parts along dimension 0, may hold values from 1 to 6
- top_src: int32 [28, 6], P('grp'), parts along dimension 0, may hold values from 0 to 7, as said below
- top_count: int32 [28], P('grp'), parts along dimension 0, may hold values from 1 to 6
Outputs:
- potential: float32 [32, 131072], P(None, ('grp', 'br', 'sub')), parts along dimension 1
The draws below stay inside these ranges and needn't reach their ends.
There are 2 independent parts, one for each index of `grp`. The reference program is written for one: setup_inputs(seed, part) draws one part's arguments, and reference() takes and returns one part's arrays. A program takes and returns all parts, laid end to end along the dimension named above; each array names one. Nothing has to cross between parts.
Inputs may be any that keep to these rules, and one draw needn't show every extreme that they name: `order`: within each branch the 8192 entries form a permutation: every input position of the branch (its first device's columns first) appears once. `near_src`: entry 0 of each list is the leaf itself; every source lies within 32 leaves of its target; entries at positions near_count or beyond are to be ignored. `far_src`: every source lies within 32 leaves of its target and differs from it; entries at positions far_count or beyond are to be ignored. `top_src`: rows 0 to 7 belong to the branches, the next 4 rows to the level above, the last 2 rows to the level above that; entries are node numbers within the row's level and never the row's own node; entries at positions top_count or beyond are to be ignored.
All inputs are finite; a program needn't handle non-finite values.
Results may differ from the reference program's by a relative error of at most 0.0047.
Values may be sent and summed in bfloat16 or wider, within the bound.
No kernel may reach another device: no remote copies, remote signals or barrier semaphores. Data moves between devices by JAX's collectives and lax.ppermute only.
A program may use at most 64 MiB of HBM per device.

```python
import math
import jax
import jax.numpy as jnp
from jax import lax

LEAF = 128
R = 64
NRHS = 32
LEAF_DEV = 32
NEAR = 27
FAR_LEAF = 6
FAR_TOP = 6
BRANCHES = 8
LEAVES = 512
POINTS = 65536
BRANCH_PTS = 8192
TOPN = 14


def pin_source(rows, leaf, target, column):
    row = rows[leaf]
    where_at = jnp.argmax(row == target).astype(jnp.int32)
    moved = row[column]
    row = row.at[where_at].set(moved)
    row = row.at[column].set(target)
    return rows.at[leaf].set(row)


def leaf_offsets(key):
    leaf_keys = jax.random.split(key, LEAVES)
    offset_pool = jnp.concatenate([jnp.arange(-LEAF_DEV, 0, dtype=jnp.int32), jnp.arange(1, LEAF_DEV + 1, dtype=jnp.int32)])
    shuffled = jax.vmap(lambda subkey: jax.random.permutation(subkey, offset_pool))(leaf_keys)
    leaves = jnp.arange(LEAVES, dtype=jnp.int32)[:, None]
    stepped = leaves + shuffled
    inside = (stepped >= 0) & (stepped < LEAVES)
    sources = jnp.where(inside, stepped, leaves - shuffled).astype(jnp.int32)
    sources = pin_source(sources, 1, 0, NEAR - 1)
    sources = pin_source(sources, LEAVES - 2, LEAVES - 1, NEAR - 1)
    return sources.astype(jnp.int32)


def bounded_counts(key, total, lowest, highest):
    counts = jax.random.randint(key, (total,), lowest, highest + 1, dtype=jnp.int32)
    position = jax.random.randint(jax.random.fold_in(key, 1), (), 0, total, dtype=jnp.int32)
    counts = counts.at[position].set(highest)
    counts = counts.at[(position + 1) % total].set(lowest)
    return counts


def draw_order(key, part):
    key = jax.random.fold_in(key, 11)
    branch_keys = jax.random.split(key, POINTS // BRANCH_PTS)
    perms = jax.vmap(lambda subkey: jax.random.permutation(subkey, BRANCH_PTS))(branch_keys)
    return perms.reshape(POINTS).astype(jnp.int32)


def draw_near_src(key, part):
    sources = leaf_offsets(key)
    leaves = jnp.arange(LEAVES, dtype=jnp.int32)[:, None]
    return jnp.concatenate([leaves, sources[:, :NEAR - 1]], axis=1).astype(jnp.int32)


def draw_far_src(key, part):
    sources = leaf_offsets(key)
    return sources[:, NEAR - 1:NEAR - 1 + FAR_LEAF].astype(jnp.int32)


def draw_near_count(key, part):
    key = jax.random.fold_in(key, 21)
    return bounded_counts(key, LEAVES, NEAR // 2 + 1, NEAR)


def draw_far_count(key, part):
    key = jax.random.fold_in(key, 23)
    return bounded_counts(key, LEAVES, 1, FAR_LEAF)


def draw_top_src(key, part):
    key = jax.random.fold_in(key, 31)
    levels = []
    for height in range(3):
        nodes = BRANCHES // 2 ** height
        shifts = jax.random.randint(jax.random.fold_in(key, height), (nodes, FAR_TOP), 1, nodes, dtype=jnp.int32)
        if height == 0:
            shifts = shifts.at[0, 0].set(nodes - 1)
        levels.append((jnp.arange(nodes, dtype=jnp.int32)[:, None] + shifts) % nodes)
    return jnp.concatenate(levels, axis=0).astype(jnp.int32)


def draw_top_count(key, part):
    key = jax.random.fold_in(key, 41)
    return bounded_counts(key, TOPN, 1, FAR_TOP)


def steps_of(rng, extent, cuts, smallest, largest):
    factor_of, own = 1.0, jax.random.fold_in(rng, 6)
    for dim, parts in cuts:
        steps = jnp.exp(jax.random.uniform(jax.random.fold_in(own, dim), (parts,), jnp.float32, smallest / len(cuts), largest / len(cuts)))
        factor_of = factor_of * jnp.repeat(steps, extent[dim] // parts).reshape([-1 if axis == dim else 1 for axis in range(len(extent))])
    return factor_of


def noise(rng, shape, width, limit, cuts=(), held_as=jnp.bfloat16):
    level = steps_of(rng, shape, cuts, -0.22, 0.18) if cuts else 1.0
    drawn = jax.random.normal(rng, shape, jnp.float32) * width * level
    return jnp.minimum(jnp.maximum(drawn, -limit), limit).astype(held_as)


def setup_inputs(seed: int = 0, part: int = 0) -> dict:
    keys = jax.random.split(jax.random.key(seed), 15)
    part_keys = jax.random.split(jax.random.fold_in(keys[14], part), 15)
    return {
        "charges": noise(part_keys[0], (NRHS, POINTS), 1.0, 6.0, ((1, 16),)),
        "order": draw_order(jax.random.fold_in(jax.random.fold_in(keys[14], part), 71), part),
        "coords": jnp.clip(1.0 * jax.random.uniform(part_keys[2], (3, POINTS), jnp.float32) ** steps_of(part_keys[2], (3, POINTS), ((1, 16),), -0.2, 0.2), 0.0, 1.0),
        "leaf_basis": noise(part_keys[3], (LEAVES, R, LEAF), LEAF ** -0.5, 0.5, ((0, 16),)),
        "leaf_transfer": noise(part_keys[4], (LEAVES, R, R), (4 * R) ** -0.5, 0.375, ((0, 16),)),
        "branch_transfer": noise(part_keys[5], (BRANCHES, R, R), R ** -0.5, 0.75, ((0, 8),)),
        "upper_transfer": noise(part_keys[6], (BRANCHES // 2, R, R), R ** -0.5, 0.75),
        "top_skeleton": jnp.clip(jax.random.uniform(part_keys[7], (3, TOPN * R), jnp.float32, 0.0, 1.0), 0.0, 1.0),
        "near_src": draw_near_src(jax.random.fold_in(jax.random.fold_in(keys[14], part), 71), part),
        "near_count": draw_near_count(jax.random.fold_in(jax.random.fold_in(keys[14], part), 71), part),
        "far_src": draw_far_src(jax.random.fold_in(jax.random.fold_in(keys[14], part), 71), part),
        "far_count": draw_far_count(jax.random.fold_in(jax.random.fold_in(keys[14], part), 71), part),
        "top_src": draw_top_src(jax.random.fold_in(jax.random.fold_in(keys[14], part), 71), part),
        "top_count": draw_top_count(jax.random.fold_in(jax.random.fold_in(keys[14], part), 71), part),
    }


length_scale = 0.25
root_three = 1.7320508075688772

def matern(sources, targets):
    gap_first = sources[..., 0, :, None] - targets[..., 0, None, :]
    gap_second = sources[..., 1, :, None] - targets[..., 1, None, :]
    gap_third = sources[..., 2, :, None] - targets[..., 2, None, :]
    squared = gap_first * gap_first + gap_second * gap_second + gap_third * gap_third
    scaled = root_three / length_scale * jnp.sqrt(squared)
    return (1.0 + scaled) * jnp.exp(-scaled)

def node_field(source_places, target_places, source_coef, live_count):
    kernel = matern(source_places, target_places[None])
    validity = (jnp.arange(source_places.shape[0], dtype=jnp.int32) < live_count).astype(jnp.float32)
    return jnp.einsum('fqp,fqn->pn', kernel * validity[:, None, None], source_coef, precision=lax.Precision.HIGHEST)

def reference(charges, order, coords, leaf_basis, leaf_transfer, branch_transfer, upper_transfer, top_skeleton, near_src, near_count, far_src, far_count, top_src, top_count):
    highest = lax.Precision.HIGHEST
    by_branch = charges.reshape(NRHS, BRANCHES, BRANCH_PTS)
    local_order = order.reshape(1, BRANCHES, BRANCH_PTS)
    tree_charges = jnp.take_along_axis(by_branch, local_order, axis=2).reshape(NRHS, LEAVES, LEAF)
    places = coords.reshape(3, LEAVES, LEAF).transpose(1, 0, 2)
    leaf_coef = jnp.einsum('lrp,nlp->lrn', leaf_basis.astype(jnp.float32), tree_charges.astype(jnp.float32)).astype(jnp.bfloat16)
    up_terms = jnp.einsum('lrs,lrn->lsn', leaf_transfer.astype(jnp.float32), leaf_coef.astype(jnp.float32))
    branch_coef = up_terms.reshape(BRANCHES, BRANCH_PTS // LEAF, R, NRHS).sum(axis=1)
    lifted = jnp.einsum('brs,brn->bsn', branch_transfer.astype(jnp.float32), branch_coef, precision=highest)
    level_one = lifted.reshape(BRANCHES // 2, 2, R, NRHS).sum(axis=1)
    level_two = jnp.einsum('prs,prn->psn', upper_transfer.astype(jnp.float32), level_one, precision=highest)
    level_two = level_two.reshape(BRANCHES // 4, 2, R, NRHS).sum(axis=1)
    skeleton = top_skeleton.reshape(3, TOPN, R).transpose(1, 0, 2)

    def level_field(coef, offset, nodes):
        sources = top_src[offset:offset + nodes]
        return jax.vmap(node_field)(skeleton[offset + sources], skeleton[offset:offset + nodes], coef[sources], top_count[offset:offset + nodes])
    field_zero = level_field(branch_coef, 0, BRANCHES)
    field_one = level_field(level_one, BRANCHES, BRANCHES // 2)
    field_two = level_field(level_two, BRANCHES + BRANCHES // 2, BRANCHES // 4)
    parents = jnp.arange(BRANCHES // 2, dtype=jnp.int32) // 2
    down_one = field_one + jnp.einsum('prs,psn->prn', upper_transfer.astype(jnp.float32), field_two[parents], precision=highest)
    branch_parents = jnp.arange(BRANCHES, dtype=jnp.int32) // 2
    down_zero = (field_zero + jnp.einsum('brs,bsn->brn', branch_transfer.astype(jnp.float32), down_one[branch_parents], precision=highest)).astype(jnp.bfloat16)
    leaf_parent = down_zero[jnp.arange(LEAVES, dtype=jnp.int32) // (BRANCH_PTS // LEAF)]
    near_valid = (jnp.arange(NEAR, dtype=jnp.int32)[None, :] < near_count[:, None]).astype(jnp.bfloat16)
    far_valid = (jnp.arange(FAR_LEAF, dtype=jnp.int32)[None, :] < far_count[:, None]).astype(jnp.bfloat16)
    block_size = math.gcd(LEAVES, 32)
    block_count = LEAVES // block_size

    def leaf_block(inputs):
        targets, near_sources, near_live, far_sources, far_live, basis_block, transfer_block, parent_block = inputs
        near_kernel = matern(places[near_sources], targets[:, None]).astype(jnp.bfloat16) * near_live[:, :, None, None]
        rows_in = tree_charges[:, near_sources].astype(jnp.float32)
        near_part = jnp.einsum('nljq,ljqp->nlp', rows_in, near_kernel.astype(jnp.float32))
        far_kernel = matern(places[far_sources][..., :R], targets[:, None, :, :R]).astype(jnp.bfloat16) * far_live[:, :, None, None]
        leaf_field = jnp.einsum('lfqp,lfqn->lpn', far_kernel.astype(jnp.float32), leaf_coef[far_sources].astype(jnp.float32))
        leaf_down = (leaf_field + jnp.einsum('lrs,lsn->lrn', transfer_block.astype(jnp.float32), parent_block.astype(jnp.float32))).astype(jnp.bfloat16)
        return near_part + jnp.einsum('lrn,lrp->nlp', leaf_down.astype(jnp.float32), basis_block.astype(jnp.float32))

    def blocked(array):
        return array.reshape((block_count, block_size) + array.shape[1:])
    potential = lax.map(leaf_block, (blocked(places), blocked(near_src), blocked(near_valid), blocked(far_src), blocked(far_valid), blocked(leaf_basis), blocked(leaf_transfer), blocked(leaf_parent)))
    return potential.transpose(1, 0, 2, 3).reshape(NRHS, POINTS)
```

```python
import functools
import math

import jax
import jax.numpy as jnp
from jax import lax
from jax.experimental import pallas as pl
from jax.experimental.pallas import tpu as pltpu
from jax.sharding import PartitionSpec as P

scale = 1.7320508075688772 / 0.25
f32 = jnp.float32
bf16 = jnp.bfloat16
HIGHEST = lax.Precision.HIGHEST
NT = (((1,), (1,)), ((), ()))
Q = 4
UNROLL = 4
FEAT = 16
CHUNK = 256
VMEM = pl.BlockSpec(memory_space=pltpu.VMEM)
SMEM = pl.BlockSpec(memory_space=pltpu.SMEM)
params = pltpu.CompilerParams(vmem_limit_bytes=50 << 20)


def profile_of(squared):
    squared = jnp.maximum(squared, 1e-12)
    scaled = squared * lax.rsqrt(squared)
    return (1.0 + scaled) * jnp.exp(-scaled)


def split(x):
    first = x.astype(bf16).astype(f32)
    rest = x - first
    second = rest.astype(bf16).astype(f32)
    return first, second, (rest - second).astype(bf16).astype(f32)


def permute_step(c, rows, order, base, start, rhs):
    per = CHUNK // order.shape[1]
    where_from = jnp.concatenate([order[pl.ds(c * per + i, 1), :] for i in range(per)], axis=1) - base
    low = where_from & (CHUNK - 1)
    high = where_from >> (CHUNK.bit_length() - 1)
    one_hot = jnp.where(
        lax.broadcasted_iota(jnp.int32, (CHUNK, CHUNK), 0) == low, 1.0, 0.0
    ).astype(bf16)
    picked = jnp.dot(rows[...], one_hot, preferred_element_type=f32)
    found = start
    for h in range(rows.shape[0] // rhs):
        found = jnp.where(high == h, picked[h * rhs : (h + 1) * rhs], found)
    return found


def prepare(
    near_src, near_count, charges, order, coords, part, feats, target, near_tab, far_tab, counts, rows, wide, tall
):
    leaves, points = order.shape
    rhs = charges.shape[0]
    near = near_src.shape[1]
    device = lax.axis_index(("br", "sub"))
    first = device * leaves
    base = lax.axis_index("sub") * (leaves * points)
    blocks = charges.shape[1] // CHUNK
    for h in range(blocks):
        rows[h * rhs : (h + 1) * rhs, :] = charges[:, h * CHUNK : (h + 1) * CHUNK]
    place = (coords[...] - 0.5) * scale
    r1, r2, r3 = split(place)
    n1, n2, n3 = split(
        place[0:1] * place[0:1] + place[1:2] * place[1:2] + place[2:3] * place[2:3]
    )
    one = jnp.ones_like(n1)
    wide[...] = jnp.zeros_like(wide)
    wide[0:3, :] = -2.0 * r1
    wide[3:6, :] = -2.0 * r2
    wide[6:9, :] = -2.0 * r3
    wide[9:10, :] = n1
    wide[10:11, :] = n2
    wide[11:12, :] = n3
    wide[12:13, :] = one
    feats[...] = wide[...].astype(bf16)
    tall[...] = jnp.zeros_like(tall)
    for i in range(3):
        tall[3 * i : 3 * i + 3, :] = r1
        tall[9 + i : 10 + i, :] = one
    tall[12:13, :] = n1
    tall[16:19, :] = r2
    tall[19:22, :] = r2
    tall[28:29, :] = n2
    tall[32:35, :] = r3
    tall[44:45, :] = n3
    lead = 4 * Q
    for i in range(lead):
        near_tab[i] = leaves
        far_tab[i] = 3 * leaves
    per = CHUNK // points

    def step(c, ends):
        near_end, far_end = ends
        at = pl.multiple_of(c * CHUNK, CHUNK)
        found = permute_step(c, rows, order, base, jnp.zeros((rhs, CHUNK), f32), rhs)
        part[:, pl.ds(at, CHUNK)] = found.astype(bf16)
        for i in range(per):
            leaf = c * per + i
            col = pl.multiple_of(leaf * points, points)
            target[pl.ds(col, points), :] = tall[:, pl.ds(col, points)].T.astype(bf16)
            code = leaf * 128
            live = near_count[leaf]
            for j in range(near):
                offset = near_src[leaf, j] - first
                valid = j < live
                local = (offset >= 0) & (offset < leaves)
                near_tab[near_end] = code + offset
                far_tab[far_end] = code + offset + leaves
                near_end = near_end + jnp.where(local & valid, 1, 0)
                far_end = far_end + jnp.where(valid & jnp.logical_not(local), 1, 0)
            near_tab[near_end] = code + leaves
            far_tab[far_end] = code + 3 * leaves
            near_end = near_end + (near_end & 1)
            far_end = far_end + (far_end & 1)
        return near_end, far_end

    near_end, far_end = lax.fori_loop(0, blocks, step, (jnp.int32(lead), jnp.int32(lead)))
    counts[0] = (near_end - lead) >> 1
    counts[1] = (far_end - lead) >> 1

    def fill(i, _):
        near_tab[near_end + i] = leaves
        far_tab[far_end + i] = 3 * leaves
        return 0

    lax.fori_loop(0, tail_length(), fill, 0)


def tail_length():
    return 2 * Q * (UNROLL + 4)


def table_length(leaves, near):
    need = 4 * Q + leaves * (near + near % 2) + tail_length()
    return -(-need // 128) * 128


def upward(part, charges, order, feats, basis, transfer, branch_transfer, upper_transfer, pack, up, rows):
    leaves, points = order.shape
    rhs = charges.shape[0]
    rank = basis.shape[1]
    base = (1 - lax.axis_index("sub")) * (leaves * points)
    blocks = charges.shape[1] // CHUNK
    for h in range(blocks):
        rows[h * rhs : (h + 1) * rhs, :] = charges[:, h * CHUNK : (h + 1) * CHUNK]
    pack[rhs : rhs + FEAT, :] = feats[...]

    def step(c, _):
        at = pl.multiple_of(c * CHUNK, CHUNK)
        found = permute_step(c, rows, order, base, part[:, pl.ds(at, CHUNK)].astype(f32), rhs)
        pack[0:rhs, pl.ds(at, CHUNK)] = found.astype(bf16)
        return 0

    lax.fori_loop(0, blocks, step, 0)
    lane = lax.broadcasted_iota(jnp.int32, (rhs, 2 * rank), 1)
    total = jnp.zeros((rhs, rank), f32)
    half = rhs // 2
    for i in range(leaves // 2):
        two = jnp.concatenate(
            [pack[0:rhs, (2 * i + k) * points : (2 * i + k + 1) * points] for k in range(2)], axis=0
        )
        weights = basis[2 * i : 2 * i + 2].reshape(2 * rank, points)
        both = lax.dot_general(two, weights, NT, preferred_element_type=f32)
        coef = jnp.where(lane < rank, both[:rhs], both[rhs:]).astype(bf16)
        at = i * 2 * rank
        pack[rhs + FEAT : rhs + FEAT + half, at : at + 2 * rank] = coef[:half]
        pack[rhs + FEAT : rhs + FEAT + half, leaves * rank + at : leaves * rank + at + 2 * rank] = coef[half:]
        total += jnp.dot(
            coef, transfer[2 * i : 2 * i + 2].reshape(2 * rank, rank), preferred_element_type=f32
        )
    lifted = jnp.dot(total, branch_transfer[0].astype(f32), precision=HIGHEST)
    parent = lax.axis_index("br") // 2
    second = jnp.dot(lifted, upper_transfer[parent].astype(f32), precision=HIGHEST)
    up[0:rhs, 0:rank] = total
    up[0:rhs, rank : 2 * rank] = lifted
    up[rhs : rhs + half, 0:rank] = second[:half]
    up[rhs : rhs + half, rank : 2 * rank] = second[half:]


def near_items(tab, pairs, target, sources, values, out, distances, kernels, points):
    total = (pairs + Q - 1) // Q
    for ref in distances + kernels:
        ref[...] = jnp.zeros_like(ref)

    def columns(leaf):
        return pl.ds(pl.multiple_of(leaf * points, points), points)

    def decode(item, q):
        one, two = tab[(item * Q + q) * 2], tab[(item * Q + q) * 2 + 1]
        return columns(one >> 7), columns(one & 127), columns(two & 127)

    def measure(item, distance):
        for q in range(Q):
            leaf, one, two = decode(item, q)
            pair = jnp.concatenate([sources[:, one], sources[:, two]], axis=1)
            distance[:, 2 * q * points : 2 * (q + 1) * points] = jnp.dot(
                target[leaf, :], jnp.concatenate([pair, pair, pair], axis=0), preferred_element_type=f32
            )

    def apply(item, kernel):
        sums = []
        for q in range(Q):
            leaf, one, two = decode(item, q)
            pair = jnp.concatenate([values[:, one], values[:, two]], axis=1)
            sums.append(
                (
                    leaf,
                    lax.dot_general(
                        pair,
                        kernel[:, 2 * q * points : 2 * (q + 1) * points],
                        NT,
                        preferred_element_type=f32,
                    ),
                )
            )
        for leaf, value in sums:
            out[:, leaf] += value

    def step(i, _):
        for u in range(UNROLL):
            item = i * UNROLL + u
            behind, last = (u - 1) % UNROLL, (u - 2) % UNROLL
            apply(item, kernels[last])
            kernels[behind][...] = profile_of(distances[behind][...]).astype(bf16)
            measure(item + 2, distances[u])
        return 0

    lax.fori_loop(0, (total + 2 + UNROLL - 1) // UNROLL, step, 0)


def near_local(tab, counts, pack, target, out, sources, values, *scratch):
    rhs, width = out.shape
    leaves = width // 128
    sources[:, :width] = pack[rhs : rhs + FEAT, :]
    sources[:, width:] = jnp.zeros_like(sources[:, width:])
    values[:, :width] = pack[0:rhs, :]
    values[:, width:] = jnp.zeros_like(values[:, width:])
    out[...] = jnp.zeros_like(out)
    near_items(
        tab, counts[0], target, sources, values, out, scratch[:UNROLL], scratch[UNROLL:], width // leaves
    )


def near_remote(
    tab, counts, far_src, far_count, before, pack, after, target, start, out, field,
    sources, values, low_sources, high_sources, low_values, high_values, *scratch
):
    rhs, width = out.shape
    leaves, far = far_src.shape
    points = width // leaves
    rank = field.shape[1] // leaves
    half = rhs // 2
    end = 3 * width
    for k, ref in enumerate((before, pack, after)):
        sources[:, k * width : (k + 1) * width] = ref[rhs : rhs + FEAT, :]
        values[:, k * width : (k + 1) * width] = ref[0:rhs, :]
    for ref in (sources, values, low_sources, high_sources, low_values, high_values):
        ref[:, end:] = jnp.zeros_like(ref[:, end:])
    out[...] = start[...]
    near_items(tab, counts[1], target, sources, values, out, scratch[:UNROLL], scratch[UNROLL:], points)
    early = lax.broadcasted_iota(jnp.int32, (FEAT, points), 1) < rank
    early_values = lax.broadcasted_iota(jnp.int32, (rhs, points), 1) < rank
    for k, ref in enumerate((before, pack, after)):
        for i in range(leaves // 2):
            at = i * points
            block = jnp.concatenate(
                [
                    ref[rhs + FEAT : rhs + FEAT + half, at : at + points],
                    ref[rhs + FEAT : rhs + FEAT + half, leaves * rank + at : leaves * rank + at + points],
                ],
                axis=0,
            ).astype(f32)
            turned = pltpu.roll(block, rank, 1)
            to = k * width + 2 * i * points
            low_values[:, to : to + points] = jnp.where(early_values, block, 0.0).astype(bf16)
            high_values[:, to : to + points] = jnp.where(early_values, 0.0, turned).astype(bf16)
            to += points
            low_values[:, to : to + points] = jnp.where(early_values, turned, 0.0).astype(bf16)
            high_values[:, to : to + points] = jnp.where(early_values, 0.0, block).astype(bf16)
        for i in range(leaves):
            to = k * width + i * points
            block = ref[rhs : rhs + FEAT, i * points : (i + 1) * points].astype(f32)
            turned = pltpu.roll(block, rank, 1)
            low_sources[:, to : to + points] = jnp.where(early, block, 0.0).astype(bf16)
            high_sources[:, to : to + points] = jnp.where(early, 0.0, turned).astype(bf16)
    base = (lax.axis_index(("br", "sub")) - 1) * leaves
    groups = (far + 1) // 2

    def columns(leaf):
        return pl.ds(pl.multiple_of(leaf * points, points), points)

    def far_leaf(leaf):
        live = far_count[leaf]
        places, coefs = [], []
        for g in range(groups):
            picked = []
            for j in (2 * g, 2 * g + 1):
                if j < far:
                    picked.append(jnp.where(j < live, far_src[leaf, j] - base, 3 * leaves))
                else:
                    picked.append(jnp.int32(3 * leaves))
            one, two = columns(picked[0]), columns(picked[1])
            places.append(low_sources[:, one] + high_sources[:, two])
            coefs.append(low_values[:, one] + high_values[:, two])
        places = jnp.concatenate(places, axis=1)
        rows = target[pl.ds(pl.multiple_of(leaf * points, points), rank), :]
        distance = jnp.dot(rows, jnp.concatenate([places] * 3, axis=0), preferred_element_type=f32)
        return profile_of(distance).astype(bf16), jnp.concatenate(coefs, axis=1)

    def far_step(i, _):
        for u in range(4):
            pair = i * 4 + u
            kernel_one, coef_one = far_leaf(2 * pair)
            kernel_two, coef_two = far_leaf(2 * pair + 1)
            both = lax.dot_general(
                jnp.concatenate([coef_one, coef_two], axis=0),
                jnp.concatenate([kernel_one, kernel_two], axis=0),
                NT,
                preferred_element_type=f32,
            )
            field[:, columns(pair)] = jnp.where(early_values, both[:rhs], both[rhs:])
        return 0

    lax.fori_loop(0, leaves // 8, far_step, 0)


def downward(
    top_src, top_count, every, skeleton, near, field, basis, transfer, branch_transfer, upper_transfer, out, places
):
    rhs = near.shape[0]
    leaves, rank, points = basis.shape
    subs = lax.axis_size("sub")
    branches = lax.axis_size("br")
    branch = lax.axis_index("br")
    depth = every.shape[0] // (branches * subs)
    half = rhs // 2
    fan = top_src.shape[1]

    def node_places(node):
        both = skeleton[:, pl.ds(pl.multiple_of((node >> 1) * (2 * rank), 2 * rank), 2 * rank)]
        return jnp.where((node & 1) == 1, both[:, rank:], both[:, :rank])

    def coefficients(level, node):
        devices = subs << level
        first = node * devices
        total = None
        for d in range(devices):
            at = pl.multiple_of((first + d) * depth, 8)
            if level < 2:
                block = every[pl.ds(at, rhs), :]
            else:
                block = every[pl.ds(at + rhs, half), :]
            total = block if total is None else total + block
        if level == 0:
            return total[:, :rank]
        if level == 1:
            return total[:, rank:]
        return jnp.concatenate([total[:, :rank], total[:, rank:]], axis=0)

    offset = 0
    fields = []
    for level in range(3):
        node = branch >> level
        row = offset + node
        places[0:3, 0:rank] = node_places(row)
        own = places[...].T
        kernels, coefs = [], []
        for j in range(fan):
            source = top_src[row, j]
            there = node_places(offset + source)
            squared = None
            for d in range(3):
                gap = (there[d : d + 1, :] - own[0:rank, d : d + 1]) * scale
                squared = gap * gap if squared is None else squared + gap * gap
            kernels.append(profile_of(squared))
            coefs.append(jnp.where(j < top_count[row], coefficients(level, source), 0.0))
        fields.append(
            lax.dot_general(
                jnp.concatenate(coefs, axis=1),
                jnp.concatenate(kernels, axis=1),
                NT,
                precision=HIGHEST,
                preferred_element_type=f32,
            )
        )
        offset += branches >> level
    down_one = fields[1] + lax.dot_general(
        fields[2], upper_transfer[branch >> 1].astype(f32), NT, precision=HIGHEST, preferred_element_type=f32
    )
    down_zero = fields[0] + lax.dot_general(
        down_one, branch_transfer[0].astype(f32), NT, precision=HIGHEST, preferred_element_type=f32
    )
    down_zero = down_zero.astype(bf16)
    lane = lax.broadcasted_iota(jnp.int32, (rhs, 2 * rank), 1)
    for i in range(leaves // 2):
        at = 2 * i * rank
        down = field[:, at : at + 2 * rank] + lax.dot_general(
            down_zero,
            transfer[2 * i : 2 * i + 2].reshape(2 * rank, rank),
            NT,
            preferred_element_type=f32,
        )
        both = jnp.concatenate(
            [jnp.where(lane < rank, down, 0.0), jnp.where(lane < rank, 0.0, down)], axis=0
        ).astype(bf16)
        value = jnp.dot(both, basis[2 * i : 2 * i + 2].reshape(2 * rank, points), preferred_element_type=f32)
        for k in range(2):
            col = (2 * i + k) * points
            out[:, col : col + points] = near[:, col : col + points] + value[k * rhs : (k + 1) * rhs]


def shards(
    charges,
    order,
    coords,
    leaf_basis,
    leaf_transfer,
    branch_transfer,
    upper_transfer,
    top_skeleton,
    near_src,
    near_count,
    far_src,
    far_count,
    top_src,
    top_count,
):
    rhs, width = charges.shape
    leaves, rank, points = leaf_basis.shape
    near = near_src.shape[1]
    subs = lax.axis_size("sub")
    devices = lax.axis_size(("br", "sub"))
    table = table_length(leaves, near)
    shape = jax.ShapeDtypeStruct
    cost = lambda us: pl.CostEstimate(
        flops=int(us * 1e6), bytes_accessed=int(us * 3e6), transcendentals=0
    )
    own_rows = order.reshape(leaves, points)
    partner = lax.ppermute(charges, "sub", [(i, (i + 1) % subs) for i in range(subs)])
    part, feats, target, near_tab, far_tab, counts = pl.pallas_call(
        prepare,
        out_shape=(
            shape((rhs, width), bf16),
            shape((FEAT, width), bf16),
            shape((width, 3 * FEAT), bf16),
            shape((table,), jnp.int32),
            shape((table,), jnp.int32),
            shape((2,), jnp.int32),
        ),
        in_specs=[SMEM, SMEM, VMEM, VMEM, VMEM],
        out_specs=(VMEM, VMEM, VMEM, SMEM, SMEM, SMEM),
        scratch_shapes=[
            pltpu.VMEM((rhs * width // CHUNK, CHUNK), bf16),
            pltpu.VMEM((FEAT, width), f32),
            pltpu.VMEM((3 * FEAT, width), f32),
        ],
        compiler_params=params,
        cost_estimate=cost(4),
        name="prepare",
    )(near_src, near_count, charges, own_rows, coords)
    pack, up = pl.pallas_call(
        upward,
        out_shape=(shape((rhs + FEAT + rhs // 2, width), bf16), shape((rhs + rhs // 2, 2 * rank), f32)),
        in_specs=[VMEM] * 8,
        out_specs=(VMEM, VMEM),
        scratch_shapes=[pltpu.VMEM((rhs * width // CHUNK, CHUNK), bf16)],
        compiler_params=params,
        cost_estimate=cost(4),
        name="upward",
    )(part, partner, own_rows, feats, leaf_basis, leaf_transfer, branch_transfer, upper_transfer)
    every = lax.all_gather(up, ("br", "sub"), axis=0, tiled=True)
    before = lax.ppermute(pack, ("br", "sub"), [(i, i + 1) for i in range(devices - 1)])
    after = lax.ppermute(pack, ("br", "sub"), [(i + 1, i) for i in range(devices - 1)])
    pipeline = [pltpu.VMEM((points, 2 * Q * points), f32)] * UNROLL + [
        pltpu.VMEM((points, 2 * Q * points), bf16)
    ] * UNROLL
    local = pl.pallas_call(
        near_local,
        out_shape=shape((rhs, width), f32),
        in_specs=[SMEM, SMEM, VMEM, VMEM],
        out_specs=VMEM,
        scratch_shapes=[
            pltpu.VMEM((FEAT, width + points), bf16),
            pltpu.VMEM((rhs, width + points), bf16),
        ]
        + pipeline,
        compiler_params=params,
        cost_estimate=cost(12),
        name="near_local",
    )(near_tab, counts, pack, target)
    both, field = pl.pallas_call(
        near_remote,
        out_shape=(shape((rhs, width), f32), shape((rhs, leaves * rank), f32)),
        in_specs=[SMEM] * 4 + [VMEM] * 5,
        out_specs=(VMEM, VMEM),
        scratch_shapes=[
            pltpu.VMEM((FEAT, 3 * width + points), bf16),
            pltpu.VMEM((rhs, 3 * width + points), bf16),
            pltpu.VMEM((FEAT, 3 * width + points), bf16),
            pltpu.VMEM((FEAT, 3 * width + points), bf16),
            pltpu.VMEM((rhs, 3 * width + points), bf16),
            pltpu.VMEM((rhs, 3 * width + points), bf16),
        ]
        + pipeline,
        compiler_params=params,
        cost_estimate=cost(14),
        name="near_remote",
    )(far_tab, counts, far_src, far_count, before, pack, after, target, local)
    return pl.pallas_call(
        downward,
        out_shape=shape((rhs, width), f32),
        in_specs=[SMEM, SMEM] + [VMEM] * 8,
        out_specs=VMEM,
        scratch_shapes=[pltpu.VMEM((8, 128), f32)],
        compiler_params=params,
        cost_estimate=cost(4),
        name="downward",
    )(
        top_src,
        top_count,
        every,
        top_skeleton,
        both,
        field,
        leaf_basis,
        leaf_transfer,
        branch_transfer,
        upper_transfer,
    )


def solution(mesh):
    return jax.shard_map(
        shards,
        mesh=mesh,
        in_specs=(
            P(None, ("grp", "br", "sub")),
            P(("grp", "br", "sub")),
            P(None, ("grp", "br", "sub")),
            P(("grp", "br", "sub"), None, None),
            P(("grp", "br", "sub"), None, None),
            P(("grp", "br"), None, None),
            P("grp", None, None),
            P(None, "grp"),
            P(("grp", "br", "sub"), None),
            P(("grp", "br", "sub")),
            P(("grp", "br", "sub"), None),
            P(("grp", "br", "sub")),
            P("grp", None),
            P("grp"),
        ),
        out_specs=P(None, ("grp", "br", "sub")),
        check_vma=False,
    )
```

```python
import functools

import jax
import jax.numpy as jnp
from jax import lax
from jax.experimental import pallas as pl
from jax.experimental.pallas import tpu as pltpu
from jax.sharding import PartitionSpec as P

scale = 1.7320508075688772 / 0.25
f32 = jnp.float32
bf16 = jnp.bfloat16
HIGHEST = lax.Precision.HIGHEST
NT = (((1,), (1,)), ((), ()))
Q = 4
UNROLL = 4
FEAT = 16
CHUNK = 256
VMEM = pl.BlockSpec(memory_space=pltpu.VMEM)
SMEM = pl.BlockSpec(memory_space=pltpu.SMEM)
HBM = pl.BlockSpec(memory_space=pltpu.HBM)
params = pltpu.CompilerParams(vmem_limit_bytes=28 << 20)


def profile_of(squared):
    squared = jnp.maximum(squared, 1e-12)
    scaled = squared * lax.rsqrt(squared)
    return (1.0 + scaled) * jnp.exp(-scaled)


def split(x):
    first = x.astype(bf16).astype(f32)
    rest = x - first
    second = rest.astype(bf16).astype(f32)
    return first, second, (rest - second).astype(bf16).astype(f32)


def permute_step(c, rows, order, base, start, rhs):
    per = CHUNK // order.shape[1]
    where_from = jnp.concatenate([order[pl.ds(c * per + i, 1), :] for i in range(per)], axis=1) - base
    low = where_from & (CHUNK - 1)
    high = where_from >> (CHUNK.bit_length() - 1)
    one_hot = jnp.where(
        lax.broadcasted_iota(jnp.int32, (CHUNK, CHUNK), 0) == low, 1.0, 0.0
    ).astype(bf16)
    picked = jnp.dot(rows[...], one_hot, preferred_element_type=f32)
    found = start
    for h in range(rows.shape[0] // rhs):
        found = jnp.where(high == h, picked[h * rhs : (h + 1) * rhs], found)
    return found


def list_leaf(leaf, near_src, near_count, first, leaves, local, tab, end):
    code = leaf * 128
    live = near_count[leaf]
    shift = code if local else code + leaves
    for j in range(near_src.shape[1]):
        offset = near_src[leaf, j] - first
        here = (offset >= 0) & (offset < leaves)
        taken = here if local else jnp.logical_not(here)
        tab[end] = shift + offset
        end = end + jnp.where(taken & (j < live), 1, 0)
    tab[end] = code + (leaves if local else 3 * leaves)
    return end + (end & 1)


def open_list(tab, none):
    for i in range(4 * Q):
        tab[i] = none
    return jnp.int32(4 * Q)


def close_list(tab, count, end, none):
    count[0] = (end - 4 * Q) >> 1

    def fill(i, _):
        for k in range(4):
            tab[end + 4 * i + k] = none
        return 0

    lax.fori_loop(0, tail_length() // 4, fill, 0)


def prepare(*refs):
    fetched = 13
    charges_in, order_in, coords_in, near_src_in, near_count_in = refs[:5]
    sources = refs[:fetched]
    (order, near_src, near_count) = refs[fetched : fetched + 3]
    kept = refs[fetched + 3 : fetched + 11]
    part, feats, target, tab, count = refs[fetched + 11 : fetched + 16]
    charges, coords, rows, wide, tall, sems = refs[fetched + 16 :]
    copies = [
        pltpu.make_async_copy(source, dest, sems.at[i])
        for i, (source, dest) in enumerate(
            zip(sources, (charges, order, coords, near_src, near_count) + tuple(kept))
        )
    ]
    for copy in copies:
        copy.start()
    leaves, points = order.shape
    rhs = charges.shape[0]
    first = lax.axis_index(("br", "sub")) * leaves
    base = lax.axis_index("sub") * (leaves * points)
    blocks = charges.shape[1] // CHUNK
    wide[...] = jnp.zeros_like(wide)
    tall[...] = jnp.zeros_like(tall)
    copies[2].wait()
    place = (coords[...] - 0.5) * scale
    r1, r2, r3 = split(place)
    n1, n2, n3 = split(
        place[0:1] * place[0:1] + place[1:2] * place[1:2] + place[2:3] * place[2:3]
    )
    one = jnp.ones_like(n1)
    wide[0:3, :] = -2.0 * r1
    wide[3:6, :] = -2.0 * r2
    wide[6:9, :] = -2.0 * r3
    wide[9:10, :] = n1
    wide[10:11, :] = n2
    wide[11:12, :] = n3
    wide[12:13, :] = one
    feats[...] = wide[...].astype(bf16)
    for i in range(3):
        tall[3 * i : 3 * i + 3, :] = r1
        tall[9 + i : 10 + i, :] = one
    tall[12:13, :] = n1
    tall[16:19, :] = r2
    tall[19:22, :] = r2
    tall[28:29, :] = n2
    tall[32:35, :] = r3
    tall[44:45, :] = n3
    for i in (0, 1, 3, 4):
        copies[i].wait()
    for h in range(blocks):
        rows[h * rhs : (h + 1) * rhs, :] = charges[:, h * CHUNK : (h + 1) * CHUNK]
    per = CHUNK // points

    def step(c, end):
        at = pl.multiple_of(c * CHUNK, CHUNK)
        found = permute_step(c, rows, order, base, jnp.zeros((rhs, CHUNK), f32), rhs)
        part[:, pl.ds(at, CHUNK)] = found.astype(bf16)
        for i in range(per):
            leaf = c * per + i
            col = pl.multiple_of(leaf * points, points)
            target[pl.ds(col, points), :] = tall[:, pl.ds(col, points)].T.astype(bf16)
            end = list_leaf(leaf, near_src, near_count, first, leaves, True, tab, end)
        return end

    end = lax.fori_loop(0, blocks, step, open_list(tab, leaves))
    close_list(tab, count, end, leaves)
    for i in range(5, fetched):
        copies[i].wait()


def tail_length():
    return 2 * Q * (UNROLL + 4)


def table_length(leaves, near):
    need = 4 * Q + leaves * (near + near % 2) + tail_length()
    return -(-need // 128) * 128


def upward(
    near_src, near_count, part, charges, order, feats, basis, transfer, branch_transfer, upper_transfer,
    pack, up, tab, count, rows,
):
    leaves, points = order.shape
    rhs = charges.shape[0]
    rank = basis.shape[1]
    first = lax.axis_index(("br", "sub")) * leaves
    base = (1 - lax.axis_index("sub")) * (leaves * points)
    blocks = charges.shape[1] // CHUNK
    for h in range(blocks):
        rows[h * rhs : (h + 1) * rhs, :] = charges[:, h * CHUNK : (h + 1) * CHUNK]
    pack[rhs : rhs + FEAT, :] = feats[...]
    per = CHUNK // points

    def step(c, end):
        at = pl.multiple_of(c * CHUNK, CHUNK)
        found = permute_step(c, rows, order, base, part[:, pl.ds(at, CHUNK)].astype(f32), rhs)
        pack[0:rhs, pl.ds(at, CHUNK)] = found.astype(bf16)
        for i in range(per):
            end = list_leaf(c * per + i, near_src, near_count, first, leaves, False, tab, end)
        return end

    end = lax.fori_loop(0, blocks, step, open_list(tab, 3 * leaves))
    close_list(tab, count, end, 3 * leaves)
    lane = lax.broadcasted_iota(jnp.int32, (rhs, 2 * rank), 1)
    total = jnp.zeros((rhs, rank), f32)
    half = rhs // 2
    for i in range(leaves // 2):
        two = jnp.concatenate(
            [pack[0:rhs, (2 * i + k) * points : (2 * i + k + 1) * points] for k in range(2)], axis=0
        )
        weights = basis[2 * i : 2 * i + 2].reshape(2 * rank, points)
        both = lax.dot_general(two, weights, NT, preferred_element_type=f32)
        coef = jnp.where(lane < rank, both[:rhs], both[rhs:]).astype(bf16)
        at = i * 2 * rank
        pack[rhs + FEAT : rhs + FEAT + half, at : at + 2 * rank] = coef[:half]
        pack[rhs + FEAT : rhs + FEAT + half, leaves * rank + at : leaves * rank + at + 2 * rank] = coef[half:]
        total += jnp.dot(
            coef, transfer[2 * i : 2 * i + 2].reshape(2 * rank, rank), preferred_element_type=f32
        )
    lifted = jnp.dot(total, branch_transfer[0].astype(f32), precision=HIGHEST)
    parent = lax.axis_index("br") // 2
    second = jnp.dot(lifted, upper_transfer[parent].astype(f32), precision=HIGHEST)
    up[0:rhs, 0:rank] = total
    up[0:rhs, rank : 2 * rank] = lifted
    up[rhs : rhs + half, 0:rank] = second[:half]
    up[rhs : rhs + half, rank : 2 * rank] = second[half:]


def near_items(tab, begin, total, target, sources, values, out, distances, kernels, points):
    for distance, kernel in zip(distances, kernels):
        distance[...] = jnp.full(distance.shape, 1e6, f32)
        kernel[...] = jnp.zeros_like(kernel)

    def columns(leaf):
        return pl.ds(pl.multiple_of(leaf * points, points), points)

    def decode(item, q):
        at = ((begin + item) * Q + q) * 2
        one, two = tab[at], tab[at + 1]
        return columns(one >> 7), columns(one & 127), columns(two & 127)

    def measure(item, distance):
        for q in range(Q):
            leaf, one, two = decode(item, q)
            pair = jnp.concatenate([sources[:, one], sources[:, two]], axis=1)
            distance[:, 2 * q * points : 2 * (q + 1) * points] = jnp.dot(
                target[leaf, :], jnp.concatenate([pair, pair, pair], axis=0), preferred_element_type=f32
            )

    def apply(item, kernel):
        sums = []
        for q in range(Q):
            leaf, one, two = decode(item, q)
            pair = jnp.concatenate([values[:, one], values[:, two]], axis=1)
            sums.append(
                (
                    leaf,
                    lax.dot_general(
                        pair,
                        kernel[:, 2 * q * points : 2 * (q + 1) * points],
                        NT,
                        preferred_element_type=f32,
                    ),
                )
            )
        for leaf, value in sums:
            out[:, leaf] += value

    def step(i, _):
        for u in range(UNROLL):
            item = i * UNROLL + u
            behind, last = (u - 1) % UNROLL, (u - 2) % UNROLL
            apply(item, kernels[last])
            kernels[behind][...] = profile_of(distances[behind][...]).astype(bf16)
            measure(item + 2, distances[u])
        return 0

    lax.fori_loop(0, (total + 2 + UNROLL - 1) // UNROLL, step, 0)


def near_local(piece, tab, count, pack, target, *refs):
    if piece:
        start, out, sources, values, *scratch = refs
    else:
        out, sources, values, *scratch = refs
    rhs, width = out.shape
    points = sources.shape[1] - width
    sources[:, :width] = pack[rhs : rhs + FEAT, :]
    sources[:, width:] = jnp.zeros_like(sources[:, width:])
    values[:, :width] = pack[0:rhs, :]
    values[:, width:] = jnp.zeros_like(values[:, width:])
    out[...] = start[...] if piece else jnp.zeros_like(out)
    total = (count[0] + Q - 1) // Q
    first = (total // UNROLL // 2) * UNROLL + UNROLL - 2
    begin, total = (first, total - first) if piece else (0, first)
    near_items(
        tab, begin, total, target, sources, values, out, scratch[:UNROLL], scratch[UNROLL:], points
    )


def near_remote(
    tab, count, far_src, far_count, outer, inner, pack, target, start, out, field,
    sources, values, low_sources, high_sources, low_values, high_values, *scratch
):
    rhs, width = out.shape
    far, leaves = far_src.shape
    points = width // leaves
    rank = field.shape[1] // leaves
    half = rhs // 2
    end = 3 * width
    side = 2 * lax.axis_index("sub")
    windows = [(side * width, outer), ((2 - side) * width, inner), (width, pack)]
    windows = [(pl.multiple_of(at, width), ref) for at, ref in windows]
    for at, ref in windows:
        sources[:, pl.ds(at, width)] = ref[rhs : rhs + FEAT, :]
        values[:, pl.ds(at, width)] = ref[0:rhs, :]
    for ref in (sources, values, low_sources, high_sources, low_values, high_values):
        ref[:, end:] = jnp.zeros_like(ref[:, end:])
    out[...] = start[...]
    near_items(
        tab, 0, (count[0] + Q - 1) // Q, target, sources, values, out, scratch[:UNROLL], scratch[UNROLL:], points
    )
    early = lax.broadcasted_iota(jnp.int32, (FEAT, points), 1) < rank
    early_values = lax.broadcasted_iota(jnp.int32, (rhs, points), 1) < rank
    for window, ref in windows:
        for i in range(leaves // 2):
            at = i * points
            block = jnp.concatenate(
                [
                    ref[rhs + FEAT : rhs + FEAT + half, at : at + points],
                    ref[rhs + FEAT : rhs + FEAT + half, leaves * rank + at : leaves * rank + at + points],
                ],
                axis=0,
            ).astype(f32)
            turned = pltpu.roll(block, rank, 1)
            to = pl.ds(pl.multiple_of(window + 2 * i * points, points), points)
            low_values[:, to] = jnp.where(early_values, block, 0.0).astype(bf16)
            high_values[:, to] = jnp.where(early_values, 0.0, turned).astype(bf16)
            to = pl.ds(pl.multiple_of(window + (2 * i + 1) * points, points), points)
            low_values[:, to] = jnp.where(early_values, turned, 0.0).astype(bf16)
            high_values[:, to] = jnp.where(early_values, 0.0, block).astype(bf16)
        for i in range(leaves):
            to = pl.ds(pl.multiple_of(window + i * points, points), points)
            block = ref[rhs : rhs + FEAT, i * points : (i + 1) * points].astype(f32)
            turned = pltpu.roll(block, rank, 1)
            low_sources[:, to] = jnp.where(early, block, 0.0).astype(bf16)
            high_sources[:, to] = jnp.where(early, 0.0, turned).astype(bf16)
    base = (lax.axis_index(("br", "sub")) - 1) * leaves
    groups = (far + 1) // 2

    def columns(leaf):
        return pl.ds(pl.multiple_of(leaf * points, points), points)

    def far_leaf(leaf):
        live = far_count[leaf]
        places, coefs = [], []
        for g in range(groups):
            picked = []
            for j in (2 * g, 2 * g + 1):
                if j < far:
                    picked.append(jnp.where(j < live, far_src[j, leaf] - base, 3 * leaves))
                else:
                    picked.append(jnp.int32(3 * leaves))
            one, two = columns(picked[0]), columns(picked[1])
            places.append(low_sources[:, one] + high_sources[:, two])
            coefs.append(low_values[:, one] + high_values[:, two])
        places = jnp.concatenate(places, axis=1)
        rows = target[pl.ds(pl.multiple_of(leaf * points, points), rank), :]
        distance = jnp.dot(rows, jnp.concatenate([places] * 3, axis=0), preferred_element_type=f32)
        return profile_of(distance).astype(bf16), jnp.concatenate(coefs, axis=1)

    def far_step(i, _):
        for u in range(4):
            pair = i * 4 + u
            kernel_one, coef_one = far_leaf(2 * pair)
            kernel_two, coef_two = far_leaf(2 * pair + 1)
            both = lax.dot_general(
                jnp.concatenate([coef_one, coef_two], axis=0),
                jnp.concatenate([kernel_one, kernel_two], axis=0),
                NT,
                preferred_element_type=f32,
            )
            field[:, columns(pair)] = jnp.where(early_values, both[:rhs], both[rhs:])
        return 0

    lax.fori_loop(0, leaves // 8, far_step, 0)


def downward(
    top_src, top_count, mine, theirs, skeleton, near, field, basis, transfer, branch_transfer, upper_transfer, out, places, every
):
    rhs = near.shape[0]
    leaves, rank, points = basis.shape
    branches = lax.axis_size("br")
    branch = lax.axis_index("br")
    depth = every.shape[0] // branches
    half = rhs // 2
    fan = top_src.shape[0]
    every[0 : mine.shape[0], :] = mine[...]
    every[mine.shape[0] :, :] = theirs[...]
    places[...] = jnp.zeros_like(places)

    def node_places(node):
        both = skeleton[:, pl.ds(pl.multiple_of((node >> 1) * (2 * rank), 2 * rank), 2 * rank)]
        return jnp.where((node & 1) == 1, both[:, rank:], both[:, :rank])

    def coefficients(level, node):
        total = None
        for d in range(1 << level):
            at = pl.multiple_of((((node << level) + d) ^ branch) * depth, 8)
            if level < 2:
                block = every[pl.ds(at, rhs), :]
            else:
                block = every[pl.ds(at + rhs, half), :]
            total = block if total is None else total + block
        if level == 0:
            return total[:, :rank]
        if level == 1:
            return total[:, rank:]
        return jnp.concatenate([total[:, :rank], total[:, rank:]], axis=0)

    offset = 0
    fields = []
    for level in range(3):
        node = branch >> level
        row = offset + node
        places[0:3, 0:rank] = node_places(row)
        own = places[...].T
        kernels, coefs = [], []
        for j in range(fan):
            source = top_src[j, row]
            there = node_places(offset + source)
            squared = None
            for d in range(3):
                gap = (there[d : d + 1, :] - own[0:rank, d : d + 1]) * scale
                squared = gap * gap if squared is None else squared + gap * gap
            kernels.append(profile_of(squared))
            coefs.append(jnp.where(j < top_count[row], coefficients(level, source), 0.0))
        fields.append(
            lax.dot_general(
                jnp.concatenate(coefs, axis=1),
                jnp.concatenate(kernels, axis=1),
                NT,
                precision=HIGHEST,
                preferred_element_type=f32,
            )
        )
        offset += branches >> level
    down_one = fields[1] + lax.dot_general(
        fields[2], upper_transfer[branch >> 1].astype(f32), NT, precision=HIGHEST, preferred_element_type=f32
    )
    down_zero = fields[0] + lax.dot_general(
        down_one, branch_transfer[0].astype(f32), NT, precision=HIGHEST, preferred_element_type=f32
    )
    down_zero = down_zero.astype(bf16)
    lane = lax.broadcasted_iota(jnp.int32, (rhs, 2 * rank), 1)
    for i in range(leaves // 2):
        at = 2 * i * rank
        down = field[:, at : at + 2 * rank] + lax.dot_general(
            down_zero,
            transfer[2 * i : 2 * i + 2].reshape(2 * rank, rank),
            NT,
            preferred_element_type=f32,
        )
        both = jnp.concatenate(
            [jnp.where(lane < rank, down, 0.0), jnp.where(lane < rank, 0.0, down)], axis=0
        ).astype(bf16)
        value = jnp.dot(both, basis[2 * i : 2 * i + 2].reshape(2 * rank, points), preferred_element_type=f32)
        for k in range(2):
            col = (2 * i + k) * points
            out[:, col : col + points] = near[:, col : col + points] + value[k * rhs : (k + 1) * rhs]


def shards(
    charges,
    order,
    coords,
    leaf_basis,
    leaf_transfer,
    branch_transfer,
    upper_transfer,
    top_skeleton,
    near_src,
    near_count,
    far_src,
    far_count,
    top_src,
    top_count,
):
    rhs, width = charges.shape
    leaves, rank, points = leaf_basis.shape
    near = near_src.shape[1]
    branches = lax.axis_size("br")
    chips = branches
    table = table_length(leaves, near)
    shape = jax.ShapeDtypeStruct
    like = lambda x: shape(x.shape, x.dtype)
    cost = lambda us: pl.CostEstimate(
        flops=int(us * 1e6), bytes_accessed=int(us * 3e6), transcendentals=0
    )
    swap = [(0, 1), (1, 0)]
    rows = pltpu.VMEM((rhs * width // CHUNK, CHUNK), bf16)
    order = order.reshape(leaves, points)
    partner = lax.ppermute(charges, "sub", swap)
    fetched = [
        charges, order, coords, near_src, near_count,
        leaf_basis, leaf_transfer, branch_transfer, upper_transfer, top_skeleton,
        far_src.T, far_count, top_src.T,
    ]
    (
        order, near_src, near_count,
        leaf_basis, leaf_transfer, branch_transfer, upper_transfer, top_skeleton,
        far_src, far_count, top_src,
        part, feats, target, near_tab, near_pairs,
    ) = pl.pallas_call(
        prepare,
        out_shape=tuple(like(x) for i, x in enumerate(fetched) if i not in (0, 2))
        + (
            shape((rhs, width), bf16),
            shape((FEAT, width), bf16),
            shape((width, 3 * FEAT), bf16),
            shape((table,), jnp.int32),
            shape((1,), jnp.int32),
        ),
        in_specs=[HBM] * len(fetched),
        out_specs=(VMEM, SMEM, SMEM) + (VMEM,) * 5 + (SMEM,) * 3 + (VMEM, VMEM, VMEM, SMEM, SMEM),
        scratch_shapes=[
            pltpu.VMEM(charges.shape, bf16),
            pltpu.VMEM(coords.shape, f32),
            rows,
            pltpu.VMEM((FEAT, width), f32),
            pltpu.VMEM((3 * FEAT, width), f32),
            pltpu.SemaphoreType.DMA((len(fetched),)),
        ],
        compiler_params=params,
        cost_estimate=cost(4),
        name="prepare",
    )(*(pltpu.with_memory_space_constraint(x, pltpu.HBM) for x in fetched))
    pack, up, far_tab, far_pairs = pl.pallas_call(
        upward,
        out_shape=(
            shape((rhs + FEAT + rhs // 2, width), bf16),
            shape((rhs + rhs // 2, 2 * rank), f32),
            shape((table,), jnp.int32),
            shape((1,), jnp.int32),
        ),
        in_specs=[SMEM] * 2 + [VMEM] * 8,
        out_specs=(VMEM, VMEM, SMEM, SMEM),
        scratch_shapes=[rows],
        compiler_params=params,
        cost_estimate=cost(4),
        name="upward",
    )(
        near_src, near_count, part, partner, order, feats,
        leaf_basis, leaf_transfer, branch_transfer, upper_transfer,
    )
    up = up + lax.ppermute(up, "sub", swap)
    between = [(2 * j + 1, 2 * j + 2) for j in range(chips - 1)]
    outer = lax.ppermute(pack, ("br", "sub"), between + [(b, a) for a, b in between])
    inner = lax.ppermute(pack, "sub", swap)
    pipeline = [pltpu.VMEM((points, 2 * Q * points), f32)] * UNROLL + [
        pltpu.VMEM((points, 2 * Q * points), bf16)
    ] * UNROLL

    def local(piece, *start):
        return pl.pallas_call(
            functools.partial(near_local, piece),
            out_shape=shape((rhs, width), f32),
            in_specs=[SMEM, SMEM] + [VMEM] * (2 + piece),
            out_specs=VMEM,
            scratch_shapes=[
                pltpu.VMEM((FEAT, width + points), bf16),
                pltpu.VMEM((rhs, width + points), bf16),
            ]
            + pipeline,
            compiler_params=params,
            cost_estimate=cost(6),
            name="near_local",
        )(near_tab, near_pairs, pack, target, *start)

    bits = branches.bit_length() - 1
    mine = up
    both = ()
    for bit in range(bits):
        theirs = lax.ppermute(mine, "br", [(i, i ^ (1 << bit)) for i in range(branches)])
        if bit < bits - 1:
            if bit < 2:
                both = (local(bit, *both),)
                theirs, both = lax.optimization_barrier((theirs, both))
            mine = jnp.concatenate([mine, theirs], axis=0)
    both = both[0]
    both, field = pl.pallas_call(
        near_remote,
        out_shape=(shape((rhs, width), f32), shape((rhs, leaves * rank), f32)),
        in_specs=[SMEM] * 4 + [VMEM] * 5,
        out_specs=(VMEM, VMEM),
        scratch_shapes=[
            pltpu.VMEM((FEAT, 3 * width + points), bf16),
            pltpu.VMEM((rhs, 3 * width + points), bf16),
            pltpu.VMEM((FEAT, 3 * width + points), bf16),
            pltpu.VMEM((FEAT, 3 * width + points), bf16),
            pltpu.VMEM((rhs, 3 * width + points), bf16),
            pltpu.VMEM((rhs, 3 * width + points), bf16),
        ]
        + pipeline,
        compiler_params=params,
        cost_estimate=cost(14),
        name="near_remote",
    )(far_tab, far_pairs, far_src, far_count, outer, inner, pack, target, both)
    return pl.pallas_call(
        downward,
        out_shape=shape((rhs, width), f32),
        in_specs=[SMEM, SMEM] + [VMEM] * 9,
        out_specs=VMEM,
        scratch_shapes=[
            pltpu.VMEM((8, 128), f32),
            pltpu.VMEM((branches * up.shape[0], 2 * rank), f32),
        ],
        compiler_params=params,
        cost_estimate=cost(4),
        name="downward",
    )(
        top_src, top_count, mine, theirs, top_skeleton, both, field,
        leaf_basis, leaf_transfer, branch_transfer, upper_transfer,
    )


def solution(mesh):
    return jax.shard_map(
        shards,
        mesh=mesh,
        in_specs=(
            P(None, ("grp", "br", "sub")),
            P(("grp", "br", "sub")),
            P(None, ("grp", "br", "sub")),
            P(("grp", "br", "sub"), None, None),
            P(("grp", "br", "sub"), None, None),
            P(("grp", "br"), None, None),
            P("grp", None, None),
            P(None, "grp"),
            P(("grp", "br", "sub"), None),
            P(("grp", "br", "sub")),
            P(("grp", "br", "sub"), None),
            P(("grp", "br", "sub")),
            P("grp", None),
            P("grp"),
        ),
        out_specs=P(None, ("grp", "br", "sub")),
        check_vma=False,
    )
```

```python
import functools

import jax
import jax.numpy as jnp
from jax import lax
from jax.experimental import pallas as pl
from jax.experimental.pallas import tpu as pltpu
from jax.sharding import PartitionSpec as P

scale = 1.7320508075688772 / 0.25
f32 = jnp.float32
bf16 = jnp.bfloat16
HIGHEST = lax.Precision.HIGHEST
NT = (((1,), (1,)), ((), ()))
Q = 4
UNROLL = 3
WIDE = 32
FEAT = 16
CHUNK = 256
VMEM = pl.BlockSpec(memory_space=pltpu.VMEM)
SMEM = pl.BlockSpec(memory_space=pltpu.SMEM)
HBM = pl.BlockSpec(memory_space=pltpu.HBM)
params = pltpu.CompilerParams(vmem_limit_bytes=28 << 20)


def profile_of(squared):
    squared = jnp.maximum(squared, 1e-12)
    scaled = squared * lax.rsqrt(squared)
    return (1.0 + scaled) * jnp.exp(-scaled)


def split(x):
    first = x.astype(bf16).astype(f32)
    rest = x - first
    second = rest.astype(bf16).astype(f32)
    return first, second, (rest - second).astype(bf16).astype(f32)


def permute(rows, order, store, extra, hots, picks, rhs):
    per = CHUNK // order.shape[1]
    groups = rows.shape[0] // rhs
    blocks = order.shape[0] // per
    cuts = 8

    def within(c):
        return jnp.clip(c, 0, blocks - 1)

    def where_from(c):
        return jnp.concatenate([order[pl.ds(within(c) * per + i, 1), :] for i in range(per)], axis=1)

    def step(i, state):
        for u in range(2):
            c = 2 * i + u
            low = where_from(c) & (CHUNK - 1)
            high = where_from(c - 2) >> (CHUNK.bit_length() - 1)
            at = pl.ds(pl.multiple_of(within(c - 2) * CHUNK, CHUNK), CHUNK)
            found = jnp.zeros((rhs, CHUNK), f32)
            tall = rows.shape[0] // cuts
            for k in range(cuts):
                part = slice(k * tall, (k + 1) * tall)
                picks[u][part, :] = jnp.dot(rows[part, :], hots[1 - u][...], preferred_element_type=f32)
                for h in range(k * groups // cuts, (k + 1) * groups // cuts):
                    found = jnp.where(high == h, picks[1 - u][h * rhs : (h + 1) * rhs, :], found)
                lines = CHUNK // cuts
                line = lax.broadcasted_iota(jnp.int32, (lines, CHUNK), 0) + k * lines
                hots[u][k * lines : (k + 1) * lines, :] = jnp.where(line == low, 1.0, 0.0).astype(bf16)
            store(at, found.astype(bf16))
            extra(c, u, within)
        return state

    lax.fori_loop(0, (blocks + 5) // 2, step, 0)


def make_list(flag, source, none, height):
    leaves, near = flag.shape
    flags = jnp.where(flag, 1.0, 0.0)
    before = lax.broadcasted_iota(jnp.int32, (near, near), 0) < lax.broadcasted_iota(jnp.int32, (near, near), 1)
    rank = jnp.dot(flags.astype(bf16), jnp.where(before, 1.0, 0.0).astype(bf16), preferred_element_type=f32)
    number = jnp.sum(flags, axis=1, keepdims=True).astype(jnp.int32)
    even = (number + (number & 1)).astype(f32)
    above = lax.broadcasted_iota(jnp.int32, (leaves, leaves), 1) < lax.broadcasted_iota(jnp.int32, (leaves, leaves), 0)
    start = jnp.dot(
        jnp.where(above, 1.0, 0.0).astype(bf16),
        jnp.broadcast_to(even, (leaves, near)).astype(bf16),
        preferred_element_type=f32,
    )
    place = jnp.where(flag, (start + rank).astype(jnp.int32) + 4 * Q, -1)
    high, low = place >> (WIDE.bit_length() - 1), place & (WIDE - 1)
    lane = lax.broadcasted_iota(jnp.int32, (leaves, 2 * WIDE), 1)
    leaf = lax.broadcasted_iota(jnp.int32, (leaves, 2 * WIDE), 0)
    line = lax.broadcasted_iota(jnp.int32, (leaves, height), 1)
    left, right = [], []
    for j in range(near):
        left.append(jnp.where(line == high[:, j : j + 1], 1.0, 0.0).astype(bf16))
        value = jnp.where(lane < WIDE, leaf, source[:, j : j + 1] + 1)
        right.append(jnp.where((lane & (WIDE - 1)) == low[:, j : j + 1], value, 0).astype(f32).astype(bf16))
    out = lax.dot_general(
        jnp.concatenate(left, axis=0),
        jnp.concatenate(right, axis=0),
        (((0,), (0,)), ((), ())),
        preferred_element_type=f32,
    ).astype(jnp.int32)
    found = out[:, WIDE:]
    code = out[:, :WIDE] * 256 + 2 * jnp.where(found == 0, none, found - 1)
    shape = (height, WIDE)
    last = lax.broadcasted_iota(jnp.int32, shape, 0) * WIDE + lax.broadcasted_iota(jnp.int32, shape, 1)
    pairs = (jnp.sum(even, axis=0, keepdims=True) * 0.5).astype(jnp.int32)
    return jnp.where(last == height * WIDE - 1, pairs, code)


def prepare(*refs):
    fetched = 14
    sources = refs[:fetched]
    charges, order, near_tab, far_tab = refs[fetched : fetched + 4]
    kept = refs[fetched + 4 : fetched + 13]
    feats, tall = refs[fetched + 13 : fetched + 15]
    coords, near_src, near_count, wide, high, sems, coded, code_sems = refs[fetched + 15 :]
    copies = [
        pltpu.make_async_copy(source, dest, sems.at[i])
        for i, (source, dest) in enumerate(
            zip(sources, (charges, order, coords, near_src, near_count) + tuple(kept))
        )
    ]
    for copy in copies:
        copy.start()
    leaves = order.shape[0]
    first = lax.axis_index(("br", "sub")) * leaves
    for i in (3, 4):
        copies[i].wait()
    near = near_src.shape[1]
    square = (leaves, leaves)
    diagonal = lax.broadcasted_iota(jnp.int32, square, 0) == lax.broadcasted_iota(jnp.int32, square, 1)
    live = jnp.sum(jnp.where(diagonal, near_count[...], 0), axis=1, keepdims=True)
    valid = lax.broadcasted_iota(jnp.int32, (leaves, near), 1) < live
    offset = near_src[...] - first
    here = (offset >= 0) & (offset < leaves)
    height = coded.shape[1]
    coded[0] = make_list(here & valid, offset, leaves, height)
    coded[1] = make_list(jnp.logical_not(here) & valid, offset + leaves, 3 * leaves, height)
    code_copies = [
        pltpu.make_async_copy(coded.at[i], dest, code_sems.at[i]) for i, dest in enumerate((near_tab, far_tab))
    ]
    for copy in code_copies:
        copy.start()
    wide[...] = jnp.zeros_like(wide)
    high[...] = jnp.zeros_like(high)
    copies[2].wait()
    place = (coords[...] - 0.5) * scale
    r1, r2, r3 = split(place)
    n1, n2, n3 = split(
        place[0:1] * place[0:1] + place[1:2] * place[1:2] + place[2:3] * place[2:3]
    )
    one = jnp.ones_like(n1)
    wide[0:3, :] = -2.0 * r1
    wide[3:6, :] = -2.0 * r2
    wide[6:9, :] = -2.0 * r3
    wide[9:10, :] = n1
    wide[10:11, :] = n2
    wide[11:12, :] = n3
    wide[12:13, :] = one
    feats[...] = wide[...].astype(bf16)
    for i in range(3):
        high[3 * i : 3 * i + 3, :] = r1
        high[9 + i : 10 + i, :] = one
    high[12:13, :] = n1
    high[16:19, :] = r2
    high[19:22, :] = r2
    high[28:29, :] = n2
    high[32:35, :] = r3
    high[44:45, :] = n3
    tall[...] = high[...].astype(bf16)
    for copy in code_copies:
        copy.wait()
    for i in (0, 1, *range(5, fetched)):
        copies[i].wait()


def turn(tall, target):
    width = tall.shape[1]
    square = (128, 128)
    one = jnp.where(
        lax.broadcasted_iota(jnp.int32, square, 0) == lax.broadcasted_iota(jnp.int32, square, 1), 1.0, 0.0
    ).astype(bf16)
    for at in range(0, width, 128):
        target[at : at + 128, :] = lax.dot_general(
            one, tall[:, at : at + 128], NT, preferred_element_type=f32
        ).astype(bf16)


def table_height(leaves, near):
    need = 4 * Q + leaves * (near + near % 2) + 2 * Q * (UNROLL + 4) + 1
    return -(-need // (8 * WIDE)) * 8


def upward(
    charges, partner, order, feats, basis, transfer, branch_transfer, upper_transfer,
    pack, up, rows, packed, *pipes,
):
    leaves, points = order.shape
    rhs = charges.shape[0]
    rank = basis.shape[1]
    blocks = charges.shape[1] // CHUNK
    own = lax.axis_index("sub") * blocks
    for h in range(blocks):
        for at, ref in ((own + h, charges), (blocks - own + h, partner)):
            rows[pl.ds(pl.multiple_of(at * rhs, rhs), rhs), :] = ref[:, h * CHUNK : (h + 1) * CHUNK]
    pack[rhs : rhs + FEAT, :] = feats[...]
    per = CHUNK // points
    early = lax.broadcasted_iota(jnp.int32, (rhs, 2 * rank), 1) < rank
    hots, picks, raw = pipes[:2], pipes[2:4], pipes[4:]

    def columns(leaf):
        return pl.ds(pl.multiple_of(leaf * points, points), points)

    def extra(c, u, within):
        for pair in range(per // 2):
            lines = slice(2 * rhs * pair, 2 * rhs * (pair + 1))
            leaf = within(c - 4) * per + 2 * pair
            both = raw[1 - u][lines, :]
            coef = jnp.where(early, both[:rhs], both[rhs:])
            turned = pltpu.roll(coef, rank, 1)
            packed[:, columns(leaf >> 1)] = coef.astype(bf16)
            pack[rhs + FEAT :, columns(leaf)] = jnp.where(early, coef, turned).astype(bf16)
            pack[rhs + FEAT :, columns(leaf + 1)] = jnp.where(early, turned, coef).astype(bf16)
            leaf = within(c - 3) * per + 2 * pair
            raw[u][lines, :] = lax.dot_general(
                jnp.concatenate([pack[0:rhs, columns(leaf)], pack[0:rhs, columns(leaf + 1)]], axis=0),
                basis[pl.ds(leaf, 2)].reshape(2 * rank, points),
                NT,
                preferred_element_type=f32,
            )

    def store(at, found):
        pack[0:rhs, at] = found

    permute(rows, order, store, extra, hots, picks, rhs)
    half = rhs // 2
    total = jnp.dot(packed[...], transfer[...].reshape(leaves * rank, rank), preferred_element_type=f32)
    lifted = jnp.dot(total, branch_transfer[0].astype(f32), precision=HIGHEST)
    parent = lax.axis_index("br") // 2
    second = jnp.dot(lifted, upper_transfer[parent].astype(f32), precision=HIGHEST)
    up[0:rhs, 0:rank] = total
    up[0:rhs, rank : 2 * rank] = lifted
    up[rhs : rhs + half, 0:rank] = second[:half]
    up[rhs : rhs + half, rank : 2 * rank] = second[half:]


def near_items(tab, target, sources, values, out, distances, kernels, points):
    total = (tab[tab.shape[0] - 1, WIDE - 1] + Q - 1) // Q
    for distance, kernel in zip(distances, kernels):
        distance[...] = jnp.full(distance.shape, 1e6, f32)
        kernel[...] = jnp.zeros_like(kernel)

    def columns(leaf):
        return pl.ds(pl.multiple_of(leaf * points, points), points)

    def decode(item, q):
        at = (item * Q + q) * 2
        high, low = at >> (WIDE.bit_length() - 1), at & (WIDE - 1)
        one, two = tab[high, low], tab[high, low + 1]
        return columns(one >> 8), columns((one >> 1) & 127), columns((two >> 1) & 127)

    def step(i, _):
        for u in range(UNROLL):
            item = i * UNROLL + u
            behind, last = (u - 1) % UNROLL, (u - 2) % UNROLL
            for q in range(Q):
                part = slice(2 * q * points, 2 * (q + 1) * points)
                leaf, one, two = decode(item, q)
                value = lax.dot_general(
                    jnp.concatenate([values[:, one], values[:, two]], axis=1),
                    kernels[last][:, part],
                    NT,
                    preferred_element_type=f32,
                )
                kernels[behind][:, part] = profile_of(distances[behind][:, part]).astype(bf16)
                target_leaf, one, two = decode(item + 2, q)
                pair = jnp.concatenate([sources[:, one], sources[:, two]], axis=1)
                distances[u][:, part] = jnp.dot(
                    target[target_leaf, :],
                    jnp.concatenate([pair, pair, pair], axis=0),
                    preferred_element_type=f32,
                )
                out[:, leaf] += value
        return 0

    lax.fori_loop(0, (total + 2 + UNROLL - 1) // UNROLL, step, 0)


def near_local(tab, pack, target, out, sources, values, *scratch):
    rhs, width = out.shape
    points = sources.shape[1] - width
    sources[:, :width] = pack[rhs : rhs + FEAT, :]
    sources[:, width:] = jnp.zeros_like(sources[:, width:])
    values[:, :width] = pack[0:rhs, :]
    values[:, width:] = jnp.zeros_like(values[:, width:])
    out[...] = jnp.zeros_like(out)
    near_items(
        tab, target, sources, values, out, scratch[:UNROLL], scratch[UNROLL:], points
    )


def near_remote(
    tab, far_src, far_count, outer, inner, pack, target, start, out, field,
    sources, values, coefs, *scratch
):
    rhs, width = out.shape
    far, leaves = far_src.shape
    points = width // leaves
    rank = field.shape[1] // leaves
    none = 3 * leaves
    side = 2 * lax.axis_index("sub")
    for at, ref in ((side * width, outer), ((2 - side) * width, inner), (width, pack)):
        to = pl.ds(pl.multiple_of(at, width), width)
        sources[:, to] = ref[rhs : rhs + FEAT, :]
        values[:, to] = ref[0:rhs, :]
        coefs[:, to] = ref[rhs + FEAT :, :]
    for ref in (sources, values, coefs):
        ref[:, none * points :] = jnp.zeros_like(ref[:, none * points :])
    out[...] = start[...]
    distances, kernels = scratch[:UNROLL], scratch[UNROLL:]
    near_items(tab, target, sources, values, out, distances, kernels, points)
    early = lax.broadcasted_iota(jnp.int32, (FEAT, points), 1) < rank
    early_values = lax.broadcasted_iota(jnp.int32, (rhs, points), 1) < rank
    base = (lax.axis_index(("br", "sub")) - 1) * leaves

    def columns(leaf):
        return pl.ds(pl.multiple_of(leaf * points, points), points)

    def picked(leaf, j):
        if j >= far:
            return columns(none)
        return columns(jnp.where(j < far_count[leaf], far_src[j, leaf] - base, none))

    items = leaves // 2

    def far_step(i, _):
        for u in range(UNROLL):
            item = i * UNROLL + u
            behind, last = (u - 1) % UNROLL, (u - 2) % UNROLL
            done = jnp.maximum(item - 2, 0)
            ahead = jnp.minimum(item, items - 1)
            total = jnp.zeros((2 * rhs, points), f32)
            for g in range((far + 1) // 2):
                part = slice(g * points, (g + 1) * points)
                pair = []
                for leaf in (2 * done, 2 * done + 1):
                    one, two = picked(leaf, 2 * g), picked(leaf, 2 * g + 1)
                    pair.append(jnp.where(early_values, coefs[:, one], coefs[:, two]))
                total += lax.dot_general(
                    jnp.concatenate(pair, axis=0), kernels[last][:, part], NT, preferred_element_type=f32
                )
                kernels[behind][:, part] = profile_of(distances[behind][:, part]).astype(bf16)
                for k in range(2):
                    leaf = 2 * ahead + k
                    one, two = picked(leaf, 2 * g), picked(leaf, 2 * g + 1)
                    turned = pltpu.roll(sources[:, two].astype(f32), rank, 1)
                    both = jnp.where(early, sources[:, one].astype(f32), turned).astype(bf16)
                    distances[u][k * rank : (k + 1) * rank, part] = jnp.dot(
                        target[pl.ds(pl.multiple_of(leaf * points, points), rank), :],
                        jnp.concatenate([both, both, both], axis=0),
                        preferred_element_type=f32,
                    )
            field[:, columns(done)] = jnp.where(early_values, total[:rhs], total[rhs:])
        return 0

    lax.fori_loop(0, (items + 2 + UNROLL - 1) // UNROLL, far_step, 0)


def downward(
    top_src, top_count, mine, theirs, skeleton, near, field, basis, transfer, branch_transfer, upper_transfer, out, places, every
):
    rhs = near.shape[0]
    leaves, rank, points = basis.shape
    branches = lax.axis_size("br")
    branch = lax.axis_index("br")
    depth = every.shape[0] // branches
    half = rhs // 2
    fan = top_src.shape[0]
    every[0 : mine.shape[0], :] = mine[...]
    every[mine.shape[0] :, :] = theirs[...]
    places[...] = jnp.zeros_like(places)

    def node_places(node):
        both = skeleton[:, pl.ds(pl.multiple_of((node >> 1) * (2 * rank), 2 * rank), 2 * rank)]
        return jnp.where((node & 1) == 1, both[:, rank:], both[:, :rank])

    def coefficients(level, node):
        total = None
        for d in range(1 << level):
            at = pl.multiple_of((((node << level) + d) ^ branch) * depth, 8)
            if level < 2:
                block = every[pl.ds(at, rhs), :]
            else:
                block = every[pl.ds(at + rhs, half), :]
            total = block if total is None else total + block
        if level == 0:
            return total[:, :rank]
        if level == 1:
            return total[:, rank:]
        return jnp.concatenate([total[:, :rank], total[:, rank:]], axis=0)

    offset = 0
    fields = []
    for level in range(3):
        node = branch >> level
        row = offset + node
        places[0:3, 0:rank] = node_places(row)
        own = places[...].T
        kernels, coefs = [], []
        for j in range(fan):
            source = top_src[j, row]
            there = node_places(offset + source)
            squared = None
            for d in range(3):
                gap = (there[d : d + 1, :] - own[0:rank, d : d + 1]) * scale
                squared = gap * gap if squared is None else squared + gap * gap
            kernels.append(profile_of(squared))
            coefs.append(jnp.where(j < top_count[row], coefficients(level, source), 0.0))
        fields.append(
            lax.dot_general(
                jnp.concatenate(coefs, axis=1),
                jnp.concatenate(kernels, axis=1),
                NT,
                precision=HIGHEST,
                preferred_element_type=f32,
            )
        )
        offset += branches >> level
    down_one = fields[1] + lax.dot_general(
        fields[2], upper_transfer[branch >> 1].astype(f32), NT, precision=HIGHEST, preferred_element_type=f32
    )
    down_zero = fields[0] + lax.dot_general(
        down_one, branch_transfer[0].astype(f32), NT, precision=HIGHEST, preferred_element_type=f32
    )
    down_zero = down_zero.astype(bf16)
    lane = lax.broadcasted_iota(jnp.int32, (rhs, 2 * rank), 1)
    for i in range(leaves // 2):
        at = 2 * i * rank
        down = field[:, at : at + 2 * rank] + lax.dot_general(
            down_zero,
            transfer[2 * i : 2 * i + 2].reshape(2 * rank, rank),
            NT,
            preferred_element_type=f32,
        )
        both = jnp.concatenate(
            [jnp.where(lane < rank, down, 0.0), jnp.where(lane < rank, 0.0, down)], axis=0
        ).astype(bf16)
        value = jnp.dot(both, basis[2 * i : 2 * i + 2].reshape(2 * rank, points), preferred_element_type=f32)
        for k in range(2):
            col = (2 * i + k) * points
            out[:, col : col + points] = near[:, col : col + points] + value[k * rhs : (k + 1) * rhs]


def shards(
    charges,
    order,
    coords,
    leaf_basis,
    leaf_transfer,
    branch_transfer,
    upper_transfer,
    top_skeleton,
    near_src,
    near_count,
    far_src,
    far_count,
    top_src,
    top_count,
):
    rhs, width = charges.shape
    leaves, rank, points = leaf_basis.shape
    near = near_src.shape[1]
    branches = lax.axis_size("br")
    height = table_height(leaves, near)
    shape = jax.ShapeDtypeStruct
    like = lambda x: shape(x.shape, x.dtype)
    cost = lambda us: pl.CostEstimate(
        flops=int(us * 1e6), bytes_accessed=int(us * 3e6), transcendentals=0
    )
    swap = [(0, 1), (1, 0)]
    order = order.reshape(leaves, points)
    partner = lax.ppermute(charges, "sub", swap)
    fetched = [
        charges, order, coords, near_src, near_count.reshape(1, leaves),
        leaf_basis, leaf_transfer, branch_transfer, upper_transfer, top_skeleton,
        far_src.T, far_count, top_src.T, top_count,
    ]
    (
        own, order, near_tab, far_tab,
        leaf_basis, leaf_transfer, branch_transfer, upper_transfer, top_skeleton,
        far_src, far_count, top_src, top_count,
        feats, tall,
    ) = pl.pallas_call(
        prepare,
        out_shape=(like(charges), like(order), shape((height, WIDE), jnp.int32), shape((height, WIDE), jnp.int32))
        + tuple(like(x) for x in fetched[5:])
        + (shape((FEAT, width), bf16), shape((3 * FEAT, width), bf16)),
        in_specs=[HBM] * len(fetched),
        out_specs=(VMEM, VMEM, SMEM, SMEM) + (VMEM,) * 5 + (SMEM,) * 4 + (VMEM, VMEM),
        scratch_shapes=[
            pltpu.VMEM(coords.shape, f32),
            pltpu.VMEM(near_src.shape, jnp.int32),
            pltpu.VMEM((1, leaves), jnp.int32),
            pltpu.VMEM((FEAT, width), f32),
            pltpu.VMEM((3 * FEAT, width), f32),
            pltpu.SemaphoreType.DMA((len(fetched),)),
            pltpu.VMEM((2, height, WIDE), jnp.int32),
            pltpu.SemaphoreType.DMA((2,)),
        ],
        compiler_params=params,
        cost_estimate=cost(2),
        name="prepare",
    )(*(pltpu.with_memory_space_constraint(x, pltpu.HBM) for x in fetched))
    chunks = 2 * rhs * width // CHUNK
    pack, up = pl.pallas_call(
        upward,
        out_shape=(
            shape((2 * rhs + FEAT, width), bf16),
            shape((rhs + rhs // 2, 2 * rank), f32),
        ),
        in_specs=[VMEM] * 8,
        out_specs=(VMEM, VMEM),
        scratch_shapes=[
            pltpu.VMEM((chunks, CHUNK), bf16),
            pltpu.VMEM((rhs, leaves * rank), bf16),
            *[pltpu.VMEM((CHUNK, CHUNK), bf16)] * 2,
            *[pltpu.VMEM((chunks, CHUNK), f32)] * 2,
            *[pltpu.VMEM((rhs * CHUNK // points, 2 * rank), f32)] * 2,
        ],
        compiler_params=params,
        cost_estimate=cost(6),
        name="upward",
    )(
        own, partner, order, feats,
        leaf_basis, leaf_transfer, branch_transfer, upper_transfer,
    )
    target = pl.pallas_call(
        turn,
        out_shape=shape((width, 3 * FEAT), bf16),
        in_specs=[VMEM],
        out_specs=VMEM,
        compiler_params=params,
        cost_estimate=cost(1),
        name="turn",
    )(tall)
    up = up + lax.ppermute(up, "sub", swap)
    between = [(2 * j + 1, 2 * j + 2) for j in range(branches - 1)]
    up, held = lax.optimization_barrier((up, pack))
    exchange = lambda x, bit: lax.ppermute(x, "br", [(i, i ^ (1 << bit)) for i in range(branches)])
    theirs, held = lax.optimization_barrier((exchange(up, 0), held))
    outer = lax.ppermute(held, ("br", "sub"), between + [(b, a) for a, b in between])
    inner = lax.ppermute(held, "sub", swap)
    pipeline = [pltpu.VMEM((points, 2 * Q * points), f32)] * UNROLL + [
        pltpu.VMEM((points, 2 * Q * points), bf16)
    ] * UNROLL

    def local():
        return pl.pallas_call(
            near_local,
            out_shape=shape((rhs, width), f32),
            in_specs=[SMEM, VMEM, VMEM],
            out_specs=VMEM,
            scratch_shapes=[
                pltpu.VMEM((FEAT, width + points), bf16),
                pltpu.VMEM((rhs, width + points), bf16),
            ]
            + pipeline,
            compiler_params=params,
            cost_estimate=cost(11),
            name="near_local",
        )(near_tab, held, target)

    mine = up
    for bit in range(1, branches.bit_length() - 1):
        mine = jnp.concatenate([mine, theirs], axis=0)
        theirs = exchange(mine, bit)
        if bit == branches.bit_length() - 3:
            theirs, start = lax.optimization_barrier((theirs, local()))
    both, field = pl.pallas_call(
        near_remote,
        out_shape=(shape((rhs, width), f32), shape((rhs, leaves * rank), f32)),
        in_specs=[SMEM] * 3 + [VMEM] * 5,
        out_specs=(VMEM, VMEM),
        scratch_shapes=[
            pltpu.VMEM((FEAT, 3 * width + points), bf16),
            pltpu.VMEM((rhs, 3 * width + points), bf16),
            pltpu.VMEM((rhs, 3 * width + points), bf16),
        ]
        + pipeline,
        compiler_params=params,
        cost_estimate=cost(14),
        name="near_remote",
    )(far_tab, far_src, far_count, outer, inner, pack, target, start)
    return pl.pallas_call(
        downward,
        out_shape=shape((rhs, width), f32),
        in_specs=[SMEM, SMEM] + [VMEM] * 9,
        out_specs=VMEM,
        scratch_shapes=[
            pltpu.VMEM((8, 128), f32),
            pltpu.VMEM((branches * up.shape[0], 2 * rank), f32),
        ],
        compiler_params=params,
        cost_estimate=cost(4),
        name="downward",
    )(
        top_src, top_count, mine, theirs, top_skeleton, both, field,
        leaf_basis, leaf_transfer, branch_transfer, upper_transfer,
    )


def solution(mesh):
    return jax.shard_map(
        shards,
        mesh=mesh,
        in_specs=(
            P(None, ("grp", "br", "sub")),
            P(("grp", "br", "sub")),
            P(None, ("grp", "br", "sub")),
            P(("grp", "br", "sub"), None, None),
            P(("grp", "br", "sub"), None, None),
            P(("grp", "br"), None, None),
            P("grp", None, None),
            P(None, "grp"),
            P(("grp", "br", "sub"), None),
            P(("grp", "br", "sub")),
            P(("grp", "br", "sub"), None),
            P(("grp", "br", "sub")),
            P("grp", None),
            P("grp"),
        ),
        out_specs=P(None, ("grp", "br", "sub")),
        check_vma=False,
    )
```

```python
import jax
import jax.numpy as jnp
from jax import lax
from jax.experimental import pallas as pl
from jax.experimental.pallas import tpu as pltpu
from jax.sharding import PartitionSpec as P

scale = 1.7320508075688772 / 0.25
f32 = jnp.float32
bf16 = jnp.bfloat16
HIGHEST = lax.Precision.HIGHEST
NT = (((1,), (1,)), ((), ()))
Q = 4
UNROLL = 3
WIDE = 32
FEAT = 16
CHUNK = 256
VMEM = pl.BlockSpec(memory_space=pltpu.VMEM)
SMEM = pl.BlockSpec(memory_space=pltpu.SMEM)
HBM = pl.BlockSpec(memory_space=pltpu.HBM)
params = pltpu.CompilerParams(vmem_limit_bytes=28 << 20)


def profile_of(squared):
    squared = jnp.maximum(squared, 1e-12)
    scaled = squared * lax.rsqrt(squared)
    return (1.0 + scaled) * jnp.exp(-scaled)


def split(x):
    first = x.astype(bf16).astype(f32)
    rest = x - first
    second = rest.astype(bf16).astype(f32)
    return first, second, (rest - second).astype(bf16).astype(f32)


def permute(rows, order, store, extra, hots, picks, rhs):
    per = CHUNK // order.shape[1]
    groups = rows.shape[0] // rhs
    blocks = order.shape[0] // per
    cuts = 8

    def within(c):
        return jnp.clip(c, 0, blocks - 1)

    def where_from(c):
        return jnp.concatenate([order[pl.ds(within(c) * per + i, 1), :] for i in range(per)], axis=1)

    def step(i, state):
        for u in range(2):
            c = 2 * i + u
            low = where_from(c) & (CHUNK - 1)
            high = where_from(c - 2) >> (CHUNK.bit_length() - 1)
            at = pl.ds(pl.multiple_of(within(c - 2) * CHUNK, CHUNK), CHUNK)
            found = jnp.zeros((rhs, CHUNK), f32)
            tall = rows.shape[0] // cuts
            for k in range(cuts):
                part = slice(k * tall, (k + 1) * tall)
                picks[u][part, :] = jnp.dot(rows[part, :], hots[1 - u][...], preferred_element_type=f32)
                for h in range(k * groups // cuts, (k + 1) * groups // cuts):
                    found = jnp.where(high == h, picks[1 - u][h * rhs : (h + 1) * rhs, :], found)
                lines = CHUNK // cuts
                line = lax.broadcasted_iota(jnp.int32, (lines, CHUNK), 0) + k * lines
                hots[u][k * lines : (k + 1) * lines, :] = jnp.where(line == low, 1.0, 0.0).astype(bf16)
            store(at, found.astype(bf16))
            extra(c, u, within)
        return state

    lax.fori_loop(0, (blocks + 5) // 2, step, 0)


def make_lists(flags, source, nones, height):
    leaves, near = source.shape
    before = lax.broadcasted_iota(jnp.int32, (near, near), 0) < lax.broadcasted_iota(jnp.int32, (near, near), 1)
    before = jnp.where(before, 1.0, 0.0).astype(bf16)
    above = lax.broadcasted_iota(jnp.int32, (leaves, leaves), 1) < lax.broadcasted_iota(jnp.int32, (leaves, leaves), 0)
    above = jnp.where(above, 1.0, 0.0).astype(bf16)
    packed = jnp.full((leaves, near), -1, jnp.int32)
    pairs = []
    for k, flag in enumerate(flags):
        ones = jnp.where(flag, 1.0, 0.0)
        number = jnp.sum(ones, axis=1, keepdims=True).astype(jnp.int32)
        even = (number + (number & 1)).astype(f32)
        place = jnp.dot(ones.astype(bf16), before, preferred_element_type=f32) + jnp.dot(
            above, jnp.broadcast_to(even, (leaves, near)).astype(bf16), preferred_element_type=f32
        )
        place = place.astype(jnp.int32) + (4 * Q + k * height * WIDE)
        packed = jnp.where(flag, place * 128 + source + 1, packed)
        pairs.append((jnp.sum(even, axis=0, keepdims=True) * 0.5).astype(jnp.int32))
    wide = max(2 * height, 2 * WIDE)
    lane = lax.broadcasted_iota(jnp.int32, (leaves, wide), 1)
    leaf = lax.broadcasted_iota(jnp.int32, (leaves, wide), 0)
    left, right = [], []
    for j in range(near):
        entry = jnp.broadcast_to(packed[:, j : j + 1], (leaves, wide))
        place = entry >> 7
        left.append(jnp.where(lane == place >> (WIDE.bit_length() - 1), 1.0, 0.0).astype(bf16))
        value = jnp.where(lane < WIDE, leaf, entry & 127)
        right.append(jnp.where(((lane ^ place) & (WIDE - 1)) == 0, value, 0).astype(f32).astype(bf16))
    out = lax.dot_general(
        jnp.concatenate(left, axis=0),
        jnp.concatenate(right, axis=0),
        (((0,), (0,)), ((), ())),
        preferred_element_type=f32,
    ).astype(jnp.int32)
    shape = (height, WIDE)
    last = lax.broadcasted_iota(jnp.int32, shape, 0) * WIDE + lax.broadcasted_iota(jnp.int32, shape, 1)
    lists = []
    for k, none in enumerate(nones):
        lines = slice(k * height, (k + 1) * height)
        found = out[lines, WIDE : 2 * WIDE]
        code = out[lines, :WIDE] * 256 + 2 * jnp.where(found == 0, none, found - 1)
        lists.append(jnp.where(last == height * WIDE - 1, pairs[k], code))
    return lists


def prepare(*refs):
    fetched = 14
    sources = refs[:fetched]
    charges, order, near_src, near_count = refs[fetched : fetched + 4]
    kept = refs[fetched + 4 : fetched + 13]
    feats, tall = refs[fetched + 13 : fetched + 15]
    coords, wide, high, sems = refs[fetched + 15 :]
    copies = [
        pltpu.make_async_copy(source, dest, sems.at[i])
        for i, (source, dest) in enumerate(
            zip(sources, (charges, order, coords, near_src, near_count) + tuple(kept))
        )
    ]
    for copy in copies:
        copy.start()
    wide[...] = jnp.zeros_like(wide)
    high[...] = jnp.zeros_like(high)
    copies[2].wait()
    place = (coords[...] - 0.5) * scale
    r1, r2, r3 = split(place)
    n1, n2, n3 = split(
        place[0:1] * place[0:1] + place[1:2] * place[1:2] + place[2:3] * place[2:3]
    )
    one = jnp.ones_like(n1)
    wide[0:3, :] = -2.0 * r1
    wide[3:6, :] = -2.0 * r2
    wide[6:9, :] = -2.0 * r3
    wide[9:10, :] = n1
    wide[10:11, :] = n2
    wide[11:12, :] = n3
    wide[12:13, :] = one
    feats[...] = wide[...].astype(bf16)
    for i in range(3):
        high[3 * i : 3 * i + 3, :] = r1
        high[9 + i : 10 + i, :] = one
    high[12:13, :] = n1
    high[16:19, :] = r2
    high[19:22, :] = r2
    high[28:29, :] = n2
    high[32:35, :] = r3
    high[44:45, :] = n3
    tall[...] = high[...].astype(bf16)
    for i in (0, 1, *range(3, fetched)):
        copies[i].wait()


def turn(near_src, near_count, tall, near_tab, far_tab, target, coded, sems):
    leaves, near = near_src.shape
    square = (leaves, leaves)
    diagonal = lax.broadcasted_iota(jnp.int32, square, 0) == lax.broadcasted_iota(jnp.int32, square, 1)
    live = jnp.sum(jnp.where(diagonal, near_count[...], 0), axis=1, keepdims=True)
    valid = lax.broadcasted_iota(jnp.int32, (leaves, near), 1) < live
    offset = near_src[...] - lax.axis_index(("br", "sub")) * leaves
    here = (offset >= 0) & (offset < leaves)
    height = coded.shape[1]
    flags = (valid & here, valid & jnp.logical_not(here))
    source = jnp.where(here, offset, offset + leaves)
    coded[0], coded[1] = make_lists(flags, source, (leaves, 3 * leaves), height)
    copies = [pltpu.make_async_copy(coded.at[i], tab, sems.at[i]) for i, tab in enumerate((near_tab, far_tab))]
    for copy in copies:
        copy.start()
    square = (128, 128)
    one = jnp.where(
        lax.broadcasted_iota(jnp.int32, square, 0) == lax.broadcasted_iota(jnp.int32, square, 1), 1.0, 0.0
    ).astype(bf16)
    for at in range(0, tall.shape[1], 128):
        target[at : at + 128, :] = lax.dot_general(
            one, tall[:, at : at + 128], NT, preferred_element_type=f32
        ).astype(bf16)
    for copy in copies:
        copy.wait()


def node_places(skeleton, node, rank):
    both = skeleton[:, pl.ds(pl.multiple_of((node >> 1) * (2 * rank), 2 * rank), 2 * rank)]
    return jnp.where((node & 1) == 1, both[:, rank:], both[:, :rank])


def top_kernels(top_src, skeleton, tops, places):
    fan = top_src.shape[0]
    rank = tops.shape[1]
    places[...] = jnp.zeros_like(places)
    offset = 0
    for level in range(3):
        row = offset + (lax.axis_index("br") >> level)
        places[0:3, 0:rank] = node_places(skeleton, row, rank)
        own = places[...].T
        kernels = []
        for j in range(fan):
            there = node_places(skeleton, offset + top_src[j, row], rank)
            squared = None
            for d in range(3):
                gap = (there[d : d + 1, :] - own[0:rank, d : d + 1]) * scale
                squared = gap * gap if squared is None else squared + gap * gap
            kernels.append(profile_of(squared))
        tops[level] = jnp.concatenate(kernels, axis=1)
        offset += lax.axis_size("br") >> level


def table_height(leaves, near):
    need = 4 * Q + leaves * (near + near % 2) + 2 * Q * (UNROLL + 4) + 1
    return -(-need // (8 * WIDE)) * 8


def upward(
    charges, partner, order, feats, basis, transfer, branch_transfer, upper_transfer,
    pack, up, rows, packed, *pipes,
):
    leaves, points = order.shape
    rhs = charges.shape[0]
    rank = basis.shape[1]
    blocks = charges.shape[1] // CHUNK
    own = lax.axis_index("sub") * blocks
    for h in range(blocks):
        for at, ref in ((own + h, charges), (blocks - own + h, partner)):
            rows[pl.ds(pl.multiple_of(at * rhs, rhs), rhs), :] = ref[:, h * CHUNK : (h + 1) * CHUNK]
    pack[rhs : rhs + FEAT, :] = feats[...]
    per = CHUNK // points
    early = lax.broadcasted_iota(jnp.int32, (rhs, 2 * rank), 1) < rank
    hots, picks, raw = pipes[:2], pipes[2:4], pipes[4:]

    def columns(leaf):
        return pl.ds(pl.multiple_of(leaf * points, points), points)

    def extra(c, u, within):
        for pair in range(per // 2):
            lines = slice(2 * rhs * pair, 2 * rhs * (pair + 1))
            leaf = within(c - 4) * per + 2 * pair
            both = raw[1 - u][lines, :]
            coef = jnp.where(early, both[:rhs], both[rhs:])
            packed[:, columns(leaf >> 1)] = coef.astype(bf16)
            leaf = within(c - 3) * per + 2 * pair
            raw[u][lines, :] = lax.dot_general(
                jnp.concatenate([pack[0:rhs, columns(leaf)], pack[0:rhs, columns(leaf + 1)]], axis=0),
                basis[pl.ds(leaf, 2)].reshape(2 * rank, points),
                NT,
                preferred_element_type=f32,
            )

    def store(at, found):
        pack[0:rhs, at] = found

    permute(rows, order, store, extra, hots, picks, rhs)
    half = rhs // 2
    pack[rhs + FEAT :, : leaves * rank] = packed[:half, :]
    pack[rhs + FEAT :, leaves * rank :] = packed[half:, :]
    total = jnp.dot(packed[...], transfer[...].reshape(leaves * rank, rank), preferred_element_type=f32)
    lifted = jnp.dot(total, branch_transfer[0].astype(f32), precision=HIGHEST)
    parent = lax.axis_index("br") // 2
    second = jnp.dot(lifted, upper_transfer[parent].astype(f32), precision=HIGHEST)
    up[0:rhs, 0:rank] = total
    up[0:rhs, rank : 2 * rank] = lifted
    up[rhs : rhs + half, 0:rank] = second[:half]
    up[rhs : rhs + half, rank : 2 * rank] = second[half:]


def near_items(tab, target, sources, values, out, distances, kernels, points):
    total = (tab[tab.shape[0] - 1, WIDE - 1] + Q - 1) // Q
    for distance, kernel in zip(distances, kernels):
        distance[...] = jnp.full(distance.shape, 1e6, f32)
        kernel[...] = jnp.zeros_like(kernel)

    def columns(leaf):
        return pl.ds(pl.multiple_of(leaf * points, points), points)

    def decode(item, q):
        at = (item * Q + q) * 2
        high, low = at >> (WIDE.bit_length() - 1), at & (WIDE - 1)
        one, two = tab[high, low], tab[high, low + 1]
        return columns(one >> 8), columns((one >> 1) & 127), columns((two >> 1) & 127)

    def step(i, _):
        for u in range(UNROLL):
            item = i * UNROLL + u
            behind, last = (u - 1) % UNROLL, (u - 2) % UNROLL
            for q in range(Q):
                part = slice(2 * q * points, 2 * (q + 1) * points)
                leaf, one, two = decode(item, q)
                value = lax.dot_general(
                    jnp.concatenate([values[:, one], values[:, two]], axis=1),
                    kernels[last][:, part],
                    NT,
                    preferred_element_type=f32,
                )
                kernels[behind][:, part] = profile_of(distances[behind][:, part]).astype(bf16)
                target_leaf, one, two = decode(item + 2, q)
                pair = jnp.concatenate([sources[:, one], sources[:, two]], axis=1)
                distances[u][:, part] = jnp.dot(
                    target[target_leaf, :],
                    jnp.concatenate([pair, pair, pair], axis=0),
                    preferred_element_type=f32,
                )
                out[:, leaf] += value
        return 0

    lax.fori_loop(0, (total + 2 + UNROLL - 1) // UNROLL, step, 0)


def near_local(tab, pack, target, out, sources, values, *scratch):
    rhs, width = out.shape
    points = sources.shape[1] - width
    sources[:, :width] = pack[rhs : rhs + FEAT, :]
    sources[:, width:] = jnp.zeros_like(sources[:, width:])
    values[:, :width] = pack[0:rhs, :]
    values[:, width:] = jnp.zeros_like(values[:, width:])
    out[...] = jnp.zeros_like(out)
    near_items(tab, target, sources, values, out, scratch[:UNROLL], scratch[UNROLL:], points)


def near_remote(
    tab, far_src, far_count, outer, inner, pack, target, start, out, field,
    sources, values, coefs, *scratch
):
    rhs, width = out.shape
    far, leaves = far_src.shape
    points = width // leaves
    rank = field.shape[1] // leaves
    none = 3 * leaves
    side = 2 * lax.axis_index("sub")
    for at, ref in ((side * width, outer), ((2 - side) * width, inner), (width, pack)):
        to = pl.ds(pl.multiple_of(at, width), width)
        sources[:, to] = ref[rhs : rhs + FEAT, :]
        values[:, to] = ref[0:rhs, :]
    early_values = lax.broadcasted_iota(jnp.int32, (rhs, points), 1) < rank
    half = leaves * rank
    for window, ref in ((side, outer), (2 - side, inner), (1, pack)):
        for i in range(leaves // 2):
            at = i * points
            block = jnp.concatenate(
                [
                    ref[rhs + FEAT :, at : at + points].astype(f32),
                    ref[rhs + FEAT :, half + at : half + at + points].astype(f32),
                ],
                axis=0,
            )
            turned = pltpu.roll(block, rank, 1)
            for k, twice in enumerate(((block, turned), (turned, block))):
                to = pl.ds(pl.multiple_of((window * leaves + 2 * i + k) * points, points), points)
                coefs[:, to] = jnp.where(early_values, *twice).astype(bf16)
    for ref in (sources, values, coefs):
        ref[:, none * points :] = jnp.zeros_like(ref[:, none * points :])
    out[...] = start[...]
    distances, kernels = scratch[:UNROLL], scratch[UNROLL:]
    near_items(tab, target, sources, values, out, distances, kernels, points)
    early = lax.broadcasted_iota(jnp.int32, (FEAT, points), 1) < rank
    base = (lax.axis_index(("br", "sub")) - 1) * leaves

    def columns(leaf):
        return pl.ds(pl.multiple_of(leaf * points, points), points)

    def picked(leaf, j):
        if j >= far:
            return columns(none)
        return columns(jnp.where(j < far_count[leaf], far_src[j, leaf] - base, none))

    items = leaves // 2
    groups = (far + 1) // 2
    wide = groups * points

    def far_step(i, _):
        for u in range(UNROLL):
            item = i * UNROLL + u
            behind, last = (u - 1) % UNROLL, (u - 2) % UNROLL
            done = jnp.clip(item - 2, 0, items - 1)
            ahead = jnp.minimum(item, items - 1)
            pairs = [[], []]
            for k in range(2):
                for g in range(groups):
                    one, two = picked(2 * done + k, 2 * g), picked(2 * done + k, 2 * g + 1)
                    pairs[k].append(jnp.where(early_values, coefs[:, one], coefs[:, two]))
            total = lax.dot_general(
                jnp.concatenate([jnp.concatenate(pair, axis=1) for pair in pairs], axis=0),
                kernels[last][:, :wide],
                NT,
                preferred_element_type=f32,
            )
            for k in range(2):
                lines = slice(k * rank, (k + 1) * rank)
                kernels[behind][lines, :wide] = profile_of(distances[behind][lines, :wide]).astype(bf16)
                leaf = 2 * ahead + k
                places = []
                for g in range(groups):
                    one, two = picked(leaf, 2 * g), picked(leaf, 2 * g + 1)
                    turned = pltpu.roll(sources[:, two].astype(f32), rank, 1)
                    places.append(jnp.where(early, sources[:, one].astype(f32), turned).astype(bf16))
                places = jnp.concatenate(places, axis=1)
                distances[u][lines, :wide] = jnp.dot(
                    target[pl.ds(pl.multiple_of(leaf * points, points), rank), :],
                    jnp.concatenate([places] * 3, axis=0),
                    preferred_element_type=f32,
                )
            field[:, columns(done)] = jnp.where(early_values, total[:rhs], total[rhs:])
        return 0

    lax.fori_loop(0, (items + 2 + UNROLL - 1) // UNROLL, far_step, 0)


def downward(
    top_src, top_count, mine, theirs, tops, near, field, basis, transfer, branch_transfer, upper_transfer, out, every, halves
):
    rhs = near.shape[0]
    leaves, rank, points = basis.shape
    branches = lax.axis_size("br")
    branch = lax.axis_index("br")
    depth = every.shape[0] // branches
    half = rhs // 2
    fan = top_src.shape[0]
    every[0 : mine.shape[0], :] = mine[...]
    every[mine.shape[0] :, :] = theirs[...]

    def coefficients(level, node):
        total = None
        for d in range(1 << level):
            at = pl.multiple_of((((node << level) + d) ^ branch) * depth, 8)
            if level < 2:
                block = every[pl.ds(at, rhs), :]
            else:
                block = every[pl.ds(at + rhs, half), :]
            total = block if total is None else total + block
        if level == 0:
            return total[:, :rank]
        if level == 1:
            return total[:, rank:]
        return jnp.concatenate([total[:, :rank], total[:, rank:]], axis=0)

    offset = 0
    fields = []
    for level in range(3):
        node = branch >> level
        row = offset + node
        coefs = []
        for j in range(fan):
            source = top_src[j, row]
            coefs.append(jnp.where(j < top_count[row], coefficients(level, source), 0.0))
        fields.append(
            lax.dot_general(
                jnp.concatenate(coefs, axis=1),
                tops[level],
                NT,
                precision=HIGHEST,
                preferred_element_type=f32,
            )
        )
        offset += branches >> level
    down_one = fields[1] + lax.dot_general(
        fields[2], upper_transfer[branch >> 1].astype(f32), NT, precision=HIGHEST, preferred_element_type=f32
    )
    down_zero = fields[0] + lax.dot_general(
        down_one, branch_transfer[0].astype(f32), NT, precision=HIGHEST, preferred_element_type=f32
    )
    down_zero = down_zero.astype(bf16)
    down = field[...] + lax.dot_general(
        down_zero, transfer[...].reshape(leaves * rank, rank), NT, preferred_element_type=f32
    )
    early = (lax.broadcasted_iota(jnp.int32, down.shape, 1) & (2 * rank - 1)) < rank
    halves[0:rhs, :] = jnp.where(early, down, 0.0).astype(bf16)
    halves[rhs:, :] = jnp.where(early, 0.0, down).astype(bf16)
    for i in range(leaves // 2):
        at = 2 * i * rank
        value = jnp.dot(
            halves[:, at : at + 2 * rank],
            basis[2 * i : 2 * i + 2].reshape(2 * rank, points),
            preferred_element_type=f32,
        )
        for k in range(2):
            col = (2 * i + k) * points
            out[:, col : col + points] = near[:, col : col + points] + value[k * rhs : (k + 1) * rhs]


def shards(
    charges,
    order,
    coords,
    leaf_basis,
    leaf_transfer,
    branch_transfer,
    upper_transfer,
    top_skeleton,
    near_src,
    near_count,
    far_src,
    far_count,
    top_src,
    top_count,
):
    rhs, width = charges.shape
    leaves, rank, points = leaf_basis.shape
    near = near_src.shape[1]
    branches = lax.axis_size("br")
    height = table_height(leaves, near)
    shape = jax.ShapeDtypeStruct
    like = lambda x: shape(x.shape, x.dtype)
    cost = lambda us: pl.CostEstimate(
        flops=int(us * 1e6), bytes_accessed=int(us * 3e6), transcendentals=0
    )
    swap = [(0, 1), (1, 0)]
    order = order.reshape(leaves, points)
    partner = lax.ppermute(charges, "sub", swap)
    fetched = [
        charges, order, coords, near_src, near_count.reshape(1, leaves),
        leaf_basis, leaf_transfer, branch_transfer, upper_transfer, top_skeleton,
        far_src.T, far_count, top_src.T, top_count,
    ]
    (
        own, order, near_src, near_count,
        leaf_basis, leaf_transfer, branch_transfer, upper_transfer, top_skeleton,
        far_src, far_count, top_src, top_count,
        feats, tall,
    ) = pl.pallas_call(
        prepare,
        out_shape=tuple(like(x) for i, x in enumerate(fetched) if i != 2)
        + (shape((FEAT, width), bf16), shape((3 * FEAT, width), bf16)),
        in_specs=[HBM] * len(fetched),
        out_specs=(VMEM,) * 9 + (SMEM,) * 4 + (VMEM, VMEM),
        scratch_shapes=[
            pltpu.VMEM(coords.shape, f32),
            pltpu.VMEM((FEAT, width), f32),
            pltpu.VMEM((3 * FEAT, width), f32),
            pltpu.SemaphoreType.DMA((len(fetched),)),
        ],
        compiler_params=params,
        cost_estimate=cost(2),
        name="prepare",
    )(*(pltpu.with_memory_space_constraint(x, pltpu.HBM) for x in fetched))
    chunks = 2 * rhs * width // CHUNK
    pack, up = pl.pallas_call(
        upward,
        out_shape=(
            shape((rhs + FEAT + rhs // 2, width), bf16),
            shape((rhs + rhs // 2, 2 * rank), f32),
        ),
        in_specs=[VMEM] * 8,
        out_specs=(VMEM, VMEM),
        scratch_shapes=[
            pltpu.VMEM((chunks, CHUNK), bf16),
            pltpu.VMEM((rhs, leaves * rank), bf16),
            *[pltpu.VMEM((CHUNK, CHUNK), bf16)] * 2,
            *[pltpu.VMEM((chunks, CHUNK), f32)] * 2,
            *[pltpu.VMEM((rhs * CHUNK // points, 2 * rank), f32)] * 2,
        ],
        compiler_params=params,
        cost_estimate=cost(6),
        name="upward",
    )(
        own, partner, order, feats,
        leaf_basis, leaf_transfer, branch_transfer, upper_transfer,
    )
    near_tab, far_tab, target = pl.pallas_call(
        turn,
        out_shape=(shape((height, WIDE), jnp.int32),) * 2 + (shape((width, 3 * FEAT), bf16),),
        in_specs=[VMEM] * 3,
        out_specs=(SMEM, SMEM, VMEM),
        scratch_shapes=[pltpu.VMEM((2, height, WIDE), jnp.int32), pltpu.SemaphoreType.DMA((2,))],
        compiler_params=params,
        cost_estimate=cost(2),
        name="turn",
    )(near_src, near_count, tall)
    tops = pl.pallas_call(
        top_kernels,
        out_shape=shape((3, rank, top_src.shape[0] * rank), f32),
        in_specs=[SMEM, VMEM],
        out_specs=VMEM,
        scratch_shapes=[pltpu.VMEM((8, 128), f32)],
        compiler_params=params,
        cost_estimate=cost(1),
        name="top_kernels",
    )(top_src, top_skeleton)
    exchange = lambda x, bit: lax.ppermute(x, "br", [(i, i ^ (1 << bit)) for i in range(branches)])
    other, near_tab, far_tab, target = lax.optimization_barrier(
        (lax.ppermute(up, "sub", swap), near_tab, far_tab, target)
    )
    mine = up + other
    theirs, held, tops = lax.optimization_barrier((exchange(mine, 0), pack, tops))
    between = [(2 * j + 1, 2 * j + 2) for j in range(branches - 1)]
    outer = lax.ppermute(held, ("br", "sub"), between + [(b, a) for a, b in between])
    inner = lax.ppermute(held, "sub", swap)
    pipeline = [pltpu.VMEM((points, 2 * Q * points), f32)] * UNROLL + [
        pltpu.VMEM((points, 2 * Q * points), bf16)
    ] * UNROLL

    def local():
        return pl.pallas_call(
            near_local,
            out_shape=shape((rhs, width), f32),
            in_specs=[SMEM, VMEM, VMEM],
            out_specs=VMEM,
            scratch_shapes=[
                pltpu.VMEM((FEAT, width + points), bf16),
                pltpu.VMEM((rhs, width + points), bf16),
            ]
            + pipeline,
            compiler_params=params,
            cost_estimate=cost(6),
            name="near_local",
        )(near_tab, held, target)

    for bit in range(1, branches.bit_length() - 1):
        mine = jnp.concatenate([mine, theirs], axis=0)
        theirs = exchange(mine, bit)
        if bit == branches.bit_length() - 3:
            theirs, start = lax.optimization_barrier((theirs, local()))
    both, field = pl.pallas_call(
        near_remote,
        out_shape=(shape((rhs, width), f32), shape((rhs, leaves * rank), f32)),
        in_specs=[SMEM] * 3 + [VMEM] * 5,
        out_specs=(VMEM, VMEM),
        scratch_shapes=[
            pltpu.VMEM((FEAT, 3 * width + points), bf16),
            pltpu.VMEM((rhs, 3 * width + points), bf16),
            pltpu.VMEM((rhs, 3 * width + points), bf16),
        ]
        + pipeline,
        compiler_params=params,
        cost_estimate=cost(14),
        name="near_remote",
    )(far_tab, far_src, far_count, outer, inner, held, target, start)
    return pl.pallas_call(
        downward,
        out_shape=shape((rhs, width), f32),
        in_specs=[SMEM, SMEM] + [VMEM] * 9,
        out_specs=VMEM,
        scratch_shapes=[
            pltpu.VMEM((branches * up.shape[0], 2 * rank), f32),
            pltpu.VMEM((2 * rhs, leaves * rank), bf16),
        ],
        compiler_params=params,
        cost_estimate=cost(4),
        name="downward",
    )(
        top_src, top_count, mine, theirs, tops, both, field,
        leaf_basis, leaf_transfer, branch_transfer, upper_transfer,
    )


def solution(mesh):
    return jax.shard_map(
        shards,
        mesh=mesh,
        in_specs=(
            P(None, ("grp", "br", "sub")),
            P(("grp", "br", "sub")),
            P(None, ("grp", "br", "sub")),
            P(("grp", "br", "sub"), None, None),
            P(("grp", "br", "sub"), None, None),
            P(("grp", "br"), None, None),
            P("grp", None, None),
            P(None, "grp"),
            P(("grp", "br", "sub"), None),
            P(("grp", "br", "sub")),
            P(("grp", "br", "sub"), None),
            P(("grp", "br", "sub")),
            P("grp", None),
            P("grp"),
        ),
        out_specs=P(None, ("grp", "br", "sub")),
        check_vma=False,
    )
```

```python
import jax
import jax.numpy as jnp
from jax import lax
from jax.experimental import pallas as pl
from jax.experimental.pallas import tpu as pltpu
from jax.sharding import PartitionSpec as P

scale = 1.7320508075688772 / 0.25
f32 = jnp.float32
bf16 = jnp.bfloat16
HIGHEST = lax.Precision.HIGHEST
NT = (((1,), (1,)), ((), ()))
Q = 4
UNROLL = 3
WIDE = 32
FEAT = 16
CHUNK = 256
VMEM = pl.BlockSpec(memory_space=pltpu.VMEM)
SMEM = pl.BlockSpec(memory_space=pltpu.SMEM)
HBM = pl.BlockSpec(memory_space=pltpu.HBM)
params = pltpu.CompilerParams(vmem_limit_bytes=28 << 20)


def profile_of(squared):
    squared = jnp.maximum(squared, 1e-12)
    scaled = squared * lax.rsqrt(squared)
    return (1.0 + scaled) * jnp.exp(-scaled)


def split(x):
    first = x.astype(bf16).astype(f32)
    rest = x - first
    second = rest.astype(bf16).astype(f32)
    return first, second, (rest - second).astype(bf16).astype(f32)


def permute(rows, order, store, extra, hots, picks, rhs):
    per = CHUNK // order.shape[1]
    groups = rows.shape[0] // rhs
    blocks = order.shape[0] // per
    cuts = 4

    def within(c):
        return jnp.clip(c, 0, blocks - 1)

    def where_from(c):
        return jnp.concatenate([order[pl.ds(within(c) * per + i, 1), :] for i in range(per)], axis=1)

    def step(i, state):
        for u in range(2):
            c = 2 * i + u
            low = where_from(c) & (CHUNK - 1)
            high = where_from(c - 2) >> (CHUNK.bit_length() - 1)
            at = pl.ds(pl.multiple_of(within(c - 2) * CHUNK, CHUNK), CHUNK)
            found = jnp.zeros((rhs, CHUNK), f32)
            tall = rows.shape[0] // cuts
            for k in range(cuts):
                part = slice(k * tall, (k + 1) * tall)
                picks[u][part, :] = jnp.dot(rows[part, :], hots[1 - u][...], preferred_element_type=f32)
                for h in range(k * groups // cuts, (k + 1) * groups // cuts):
                    found = jnp.where(high == h, picks[1 - u][h * rhs : (h + 1) * rhs, :], found)
                lines = CHUNK // cuts
                line = lax.broadcasted_iota(jnp.int32, (lines, CHUNK), 0) + k * lines
                hots[u][k * lines : (k + 1) * lines, :] = jnp.where(line == low, 1.0, 0.0).astype(bf16)
            store(at, found.astype(bf16))
            extra(c, u, within)
        return state

    lax.fori_loop(0, (blocks + 5) // 2, step, 0)


def make_lists(flags, source, nones, height):
    leaves, near = source.shape
    before = lax.broadcasted_iota(jnp.int32, (near, near), 0) < lax.broadcasted_iota(jnp.int32, (near, near), 1)
    before = jnp.where(before, 1.0, 0.0).astype(bf16)
    above = lax.broadcasted_iota(jnp.int32, (leaves, leaves), 1) < lax.broadcasted_iota(jnp.int32, (leaves, leaves), 0)
    above = jnp.where(above, 1.0, 0.0).astype(bf16)
    packed = jnp.full((leaves, near), -1, jnp.int32)
    pairs = []
    for k, flag in enumerate(flags):
        ones = jnp.where(flag, 1.0, 0.0)
        number = jnp.sum(ones, axis=1, keepdims=True).astype(jnp.int32)
        even = (number + (number & 1)).astype(f32)
        place = jnp.dot(ones.astype(bf16), before, preferred_element_type=f32) + jnp.dot(
            above, jnp.broadcast_to(even, (leaves, near)).astype(bf16), preferred_element_type=f32
        )
        place = place.astype(jnp.int32) + (4 * Q + k * height * WIDE)
        packed = jnp.where(flag, place * 128 + source + 1, packed)
        pairs.append((jnp.sum(even, axis=0, keepdims=True) * 0.5).astype(jnp.int32))
    wide = max(2 * height, 2 * WIDE)
    lane = lax.broadcasted_iota(jnp.int32, (leaves, wide), 1)
    leaf = lax.broadcasted_iota(jnp.int32, (leaves, wide), 0)
    left, right = [], []
    for j in range(near):
        entry = jnp.broadcast_to(packed[:, j : j + 1], (leaves, wide))
        place = entry >> 7
        left.append(jnp.where(lane == place >> (WIDE.bit_length() - 1), 1.0, 0.0).astype(bf16))
        value = jnp.where(lane < WIDE, leaf, entry & 127)
        right.append(jnp.where(((lane ^ place) & (WIDE - 1)) == 0, value, 0).astype(f32).astype(bf16))
    out = lax.dot_general(
        jnp.concatenate(left, axis=0),
        jnp.concatenate(right, axis=0),
        (((0,), (0,)), ((), ())),
        preferred_element_type=f32,
    ).astype(jnp.int32)
    shape = (height, WIDE)
    last = lax.broadcasted_iota(jnp.int32, shape, 0) * WIDE + lax.broadcasted_iota(jnp.int32, shape, 1)
    lists = []
    for k, none in enumerate(nones):
        lines = slice(k * height, (k + 1) * height)
        found = out[lines, WIDE : 2 * WIDE]
        code = out[lines, :WIDE] * 256 + 2 * jnp.where(found == 0, none, found - 1)
        lists.append(jnp.where(last == height * WIDE - 1, pairs[k], code))
    return lists


def prepare(*refs):
    fetched = 14
    sources = refs[:fetched]
    charges, order, near_src, near_count = refs[fetched : fetched + 4]
    kept = refs[fetched + 4 : fetched + 13]
    feats, tall = refs[fetched + 13 : fetched + 15]
    coords, wide, high, sems = refs[fetched + 15 :]
    copies = [
        pltpu.make_async_copy(source, dest, sems.at[i])
        for i, (source, dest) in enumerate(
            zip(sources, (charges, order, coords, near_src, near_count) + tuple(kept))
        )
    ]
    for copy in copies:
        copy.start()
    wide[...] = jnp.zeros_like(wide)
    high[...] = jnp.zeros_like(high)
    copies[2].wait()
    place = (coords[...] - 0.5) * scale
    r1, r2, r3 = split(place)
    n1, n2, n3 = split(
        place[0:1] * place[0:1] + place[1:2] * place[1:2] + place[2:3] * place[2:3]
    )
    one = jnp.ones_like(n1)
    wide[0:3, :] = -2.0 * r1
    wide[3:6, :] = -2.0 * r2
    wide[6:9, :] = -2.0 * r3
    wide[9:10, :] = n1
    wide[10:11, :] = n2
    wide[11:12, :] = n3
    wide[12:13, :] = one
    feats[...] = wide[...].astype(bf16)
    for i in range(3):
        high[3 * i : 3 * i + 3, :] = r1
        high[9 + i : 10 + i, :] = one
    high[12:13, :] = n1
    high[16:19, :] = r2
    high[19:22, :] = r2
    high[28:29, :] = n2
    high[32:35, :] = r3
    high[44:45, :] = n3
    tall[...] = high[...].astype(bf16)
    for i in (0, 1, *range(3, fetched)):
        copies[i].wait()


def turn(near_src, near_count, tall, near_tab, far_tab, target, coded, sems):
    leaves, near = near_src.shape
    square = (leaves, leaves)
    diagonal = lax.broadcasted_iota(jnp.int32, square, 0) == lax.broadcasted_iota(jnp.int32, square, 1)
    live = jnp.sum(jnp.where(diagonal, near_count[...], 0), axis=1, keepdims=True)
    valid = lax.broadcasted_iota(jnp.int32, (leaves, near), 1) < live
    offset = near_src[...] - lax.axis_index(("br", "sub")) * leaves
    here = (offset >= 0) & (offset < leaves)
    height = coded.shape[1]
    flags = (valid & here, valid & jnp.logical_not(here))
    source = jnp.where(here, offset, offset + leaves)
    coded[0], coded[1] = make_lists(flags, source, (leaves, 3 * leaves), height)
    copies = [pltpu.make_async_copy(coded.at[i], tab, sems.at[i]) for i, tab in enumerate((near_tab, far_tab))]
    for copy in copies:
        copy.start()
    square = (128, 128)
    one = jnp.where(
        lax.broadcasted_iota(jnp.int32, square, 0) == lax.broadcasted_iota(jnp.int32, square, 1), 1.0, 0.0
    ).astype(bf16)
    for at in range(0, tall.shape[1], 128):
        target[at : at + 128, :] = lax.dot_general(
            one, tall[:, at : at + 128], NT, preferred_element_type=f32
        ).astype(bf16)
    for copy in copies:
        copy.wait()


def node_places(skeleton, node, rank):
    both = skeleton[:, pl.ds(pl.multiple_of((node >> 1) * (2 * rank), 2 * rank), 2 * rank)]
    return jnp.where((node & 1) == 1, both[:, rank:], both[:, :rank])


def top_kernels(top_src, skeleton, tops, places):
    fan = top_src.shape[0]
    rank = tops.shape[1]
    places[...] = jnp.zeros_like(places)
    offset = 0
    for level in range(3):
        row = offset + (lax.axis_index("br") >> level)
        places[0:3, 0:rank] = node_places(skeleton, row, rank)
        own = places[...].T
        kernels = []
        for j in range(fan):
            there = node_places(skeleton, offset + top_src[j, row], rank)
            squared = None
            for d in range(3):
                gap = (there[d : d + 1, :] - own[0:rank, d : d + 1]) * scale
                squared = gap * gap if squared is None else squared + gap * gap
            kernels.append(profile_of(squared))
        tops[level] = jnp.concatenate(kernels, axis=1)
        offset += lax.axis_size("br") >> level


def table_height(leaves, near):
    need = 4 * Q + leaves * (near + near % 2) + 2 * Q * (UNROLL + 4) + 1
    return -(-need // (8 * WIDE)) * 8


def upward(
    charges, partner, order, feats, basis, transfer, branch_transfer, upper_transfer,
    pack, up, rows, packed, *pipes,
):
    leaves, points = order.shape
    rhs = charges.shape[0]
    rank = basis.shape[1]
    blocks = charges.shape[1] // CHUNK
    own = lax.axis_index("sub") * blocks
    for h in range(blocks):
        for at, ref in ((own + h, charges), (blocks - own + h, partner)):
            rows[pl.ds(pl.multiple_of(at * rhs, rhs), rhs), :] = ref[:, h * CHUNK : (h + 1) * CHUNK]
    pack[rhs : rhs + FEAT, :] = feats[...]
    per = CHUNK // points
    early = lax.broadcasted_iota(jnp.int32, (rhs, 2 * rank), 1) < rank
    hots, picks, raw = pipes[:2], pipes[2:4], pipes[4:]

    def columns(leaf):
        return pl.ds(pl.multiple_of(leaf * points, points), points)

    def extra(c, u, within):
        for pair in range(per // 2):
            lines = slice(2 * rhs * pair, 2 * rhs * (pair + 1))
            leaf = within(c - 4) * per + 2 * pair
            both = raw[1 - u][lines, :]
            coef = jnp.where(early, both[:rhs], both[rhs:])
            packed[:, columns(leaf >> 1)] = coef.astype(bf16)
            leaf = within(c - 3) * per + 2 * pair
            raw[u][lines, :] = lax.dot_general(
                jnp.concatenate([pack[0:rhs, columns(leaf)], pack[0:rhs, columns(leaf + 1)]], axis=0),
                basis[pl.ds(leaf, 2)].reshape(2 * rank, points),
                NT,
                preferred_element_type=f32,
            )

    def store(at, found):
        pack[0:rhs, at] = found

    permute(rows, order, store, extra, hots, picks, rhs)
    half = rhs // 2
    pack[rhs + FEAT :, : leaves * rank] = packed[:half, :]
    pack[rhs + FEAT :, leaves * rank :] = packed[half:, :]
    total = jnp.dot(packed[...], transfer[...].reshape(leaves * rank, rank), preferred_element_type=f32)
    lifted = jnp.dot(total, branch_transfer[0].astype(f32), precision=HIGHEST)
    parent = lax.axis_index("br") // 2
    second = jnp.dot(lifted, upper_transfer[parent].astype(f32), precision=HIGHEST)
    up[0:rhs, 0:rank] = total
    up[0:rhs, rank : 2 * rank] = lifted
    up[rhs : rhs + half, 0:rank] = second[:half]
    up[rhs : rhs + half, rank : 2 * rank] = second[half:]


def near_items(tab, target, sources, values, out, distances, kernels, points):
    total = (tab[tab.shape[0] - 1, WIDE - 1] + Q - 1) // Q
    for distance, kernel in zip(distances, kernels):
        distance[...] = jnp.full(distance.shape, 1e6, f32)
        kernel[...] = jnp.zeros_like(kernel)

    def columns(leaf):
        return pl.ds(pl.multiple_of(leaf * points, points), points)

    def decode(item, q):
        at = (item * Q + q) * 2
        high, low = at >> (WIDE.bit_length() - 1), at & (WIDE - 1)
        one, two = tab[high, low], tab[high, low + 1]
        return columns(one >> 8), columns((one >> 1) & 127), columns((two >> 1) & 127)

    def step(i, _):
        for u in range(UNROLL):
            item = i * UNROLL + u
            behind, last = (u - 1) % UNROLL, (u - 2) % UNROLL
            for q in range(Q):
                part = slice(2 * q * points, 2 * (q + 1) * points)
                leaf, one, two = decode(item, q)
                value = lax.dot_general(
                    jnp.concatenate([values[:, one], values[:, two]], axis=1),
                    kernels[last][:, part],
                    NT,
                    preferred_element_type=f32,
                )
                kernels[behind][:, part] = profile_of(distances[behind][:, part]).astype(bf16)
                target_leaf, one, two = decode(item + 2, q)
                pair = jnp.concatenate([sources[:, one], sources[:, two]], axis=1)
                distances[u][:, part] = jnp.dot(
                    target[target_leaf, :],
                    jnp.concatenate([pair, pair, pair], axis=0),
                    preferred_element_type=f32,
                )
                out[:, leaf] += value
        return 0

    lax.fori_loop(0, (total + 2 + UNROLL - 1) // UNROLL, step, 0)


def near_local(tab, pack, target, out, sources, values, *scratch):
    rhs, width = out.shape
    points = sources.shape[1] - width
    sources[:, :width] = pack[rhs : rhs + FEAT, :]
    sources[:, width:] = jnp.zeros_like(sources[:, width:])
    values[:, :width] = pack[0:rhs, :]
    values[:, width:] = jnp.zeros_like(values[:, width:])
    out[...] = jnp.zeros_like(out)
    near_items(tab, target, sources, values, out, scratch[:UNROLL], scratch[UNROLL:], points)


def near_remote(
    tab, far_src, far_count, outer, inner, pack, target, start, out, field,
    sources, values, coefs, *scratch
):
    rhs, width = out.shape
    far, leaves = far_src.shape
    points = width // leaves
    rank = field.shape[1] // leaves
    none = 3 * leaves
    side = 2 * lax.axis_index("sub")
    for at, ref in ((side * width, outer), ((2 - side) * width, inner), (width, pack)):
        to = pl.ds(pl.multiple_of(at, width), width)
        sources[:, to] = ref[rhs : rhs + FEAT, :]
        values[:, to] = ref[0:rhs, :]
    early_values = lax.broadcasted_iota(jnp.int32, (rhs, points), 1) < rank
    half = leaves * rank
    for window, ref in ((side, outer), (2 - side, inner), (1, pack)):
        for i in range(leaves // 2):
            at = i * points
            block = jnp.concatenate(
                [
                    ref[rhs + FEAT :, at : at + points].astype(f32),
                    ref[rhs + FEAT :, half + at : half + at + points].astype(f32),
                ],
                axis=0,
            )
            turned = pltpu.roll(block, rank, 1)
            for k, twice in enumerate(((block, turned), (turned, block))):
                to = pl.ds(pl.multiple_of((window * leaves + 2 * i + k) * points, points), points)
                coefs[:, to] = jnp.where(early_values, *twice).astype(bf16)
    for ref in (sources, values, coefs):
        ref[:, none * points :] = jnp.zeros_like(ref[:, none * points :])
    out[...] = start[...]
    distances, kernels = scratch[:UNROLL], scratch[UNROLL:]
    near_items(tab, target, sources, values, out, distances, kernels, points)
    early = lax.broadcasted_iota(jnp.int32, (FEAT, points), 1) < rank
    base = (lax.axis_index(("br", "sub")) - 1) * leaves

    def columns(leaf):
        return pl.ds(pl.multiple_of(leaf * points, points), points)

    def picked(leaf, j):
        if j >= far:
            return columns(none)
        return columns(jnp.where(j < far_count[leaf], far_src[j, leaf] - base, none))

    items = leaves // 2
    groups = (far + 1) // 2
    wide = groups * points

    def far_step(i, _):
        for u in range(2 * UNROLL):
            item = 2 * i * UNROLL + u
            behind, last = (u - 1) % UNROLL, (u - 2) % UNROLL
            done = jnp.clip(item - 2, 0, items - 1)
            ahead = jnp.minimum(item, items - 1)
            pairs = [[], []]
            for k in range(2):
                for g in range(groups):
                    one, two = picked(2 * done + k, 2 * g), picked(2 * done + k, 2 * g + 1)
                    pairs[k].append(jnp.where(early_values, coefs[:, one], coefs[:, two]))
            total = lax.dot_general(
                jnp.concatenate([jnp.concatenate(pair, axis=1) for pair in pairs], axis=0),
                kernels[last][:, :wide],
                NT,
                preferred_element_type=f32,
            )
            for k in range(2):
                lines = slice(k * rank, (k + 1) * rank)
                kernels[behind][lines, :wide] = profile_of(distances[behind][lines, :wide]).astype(bf16)
                leaf = 2 * ahead + k
                places = []
                for g in range(groups):
                    one, two = picked(leaf, 2 * g), picked(leaf, 2 * g + 1)
                    turned = pltpu.roll(sources[:, two].astype(f32), rank, 1)
                    places.append(jnp.where(early, sources[:, one].astype(f32), turned).astype(bf16))
                places = jnp.concatenate(places, axis=1)
                distances[u % UNROLL][lines, :wide] = jnp.dot(
                    target[pl.ds(pl.multiple_of(leaf * points, points), rank), :],
                    jnp.concatenate([places] * 3, axis=0),
                    preferred_element_type=f32,
                )
            field[:, columns(done)] = jnp.where(early_values, total[:rhs], total[rhs:])
        return 0

    lax.fori_loop(0, (items + 2 + 2 * UNROLL - 1) // (2 * UNROLL), far_step, 0)


def downward(
    top_src, top_count, mine, theirs, tops, near, field, basis, transfer, branch_transfer, upper_transfer, out, every, halves
):
    rhs = near.shape[0]
    leaves, rank, points = basis.shape
    branches = lax.axis_size("br")
    branch = lax.axis_index("br")
    depth = every.shape[0] // branches
    half = rhs // 2
    fan = top_src.shape[0]
    every[0 : mine.shape[0], :] = mine[...]
    every[mine.shape[0] :, :] = theirs[...]

    def coefficients(level, node):
        total = None
        for d in range(1 << level):
            at = pl.multiple_of((((node << level) + d) ^ branch) * depth, 8)
            if level < 2:
                block = every[pl.ds(at, rhs), :]
            else:
                block = every[pl.ds(at + rhs, half), :]
            total = block if total is None else total + block
        if level == 0:
            return total[:, :rank]
        if level == 1:
            return total[:, rank:]
        return jnp.concatenate([total[:, :rank], total[:, rank:]], axis=0)

    offset = 0
    fields = []
    for level in range(3):
        node = branch >> level
        row = offset + node
        coefs = []
        for j in range(fan):
            source = top_src[j, row]
            coefs.append(jnp.where(j < top_count[row], coefficients(level, source), 0.0))
        fields.append(
            lax.dot_general(
                jnp.concatenate(coefs, axis=1),
                tops[level],
                NT,
                precision=HIGHEST,
                preferred_element_type=f32,
            )
        )
        offset += branches >> level
    down_one = fields[1] + lax.dot_general(
        fields[2], upper_transfer[branch >> 1].astype(f32), NT, precision=HIGHEST, preferred_element_type=f32
    )
    down_zero = fields[0] + lax.dot_general(
        down_one, branch_transfer[0].astype(f32), NT, precision=HIGHEST, preferred_element_type=f32
    )
    down_zero = down_zero.astype(bf16)
    down = field[...] + lax.dot_general(
        down_zero, transfer[...].reshape(leaves * rank, rank), NT, preferred_element_type=f32
    )
    early = (lax.broadcasted_iota(jnp.int32, down.shape, 1) & (2 * rank - 1)) < rank
    halves[0:rhs, :] = jnp.where(early, down, 0.0).astype(bf16)
    halves[rhs:, :] = jnp.where(early, 0.0, down).astype(bf16)
    for i in range(leaves // 2):
        at = 2 * i * rank
        value = jnp.dot(
            halves[:, at : at + 2 * rank],
            basis[2 * i : 2 * i + 2].reshape(2 * rank, points),
            preferred_element_type=f32,
        )
        for k in range(2):
            col = (2 * i + k) * points
            out[:, col : col + points] = near[:, col : col + points] + value[k * rhs : (k + 1) * rhs]


def shards(
    charges,
    order,
    coords,
    leaf_basis,
    leaf_transfer,
    branch_transfer,
    upper_transfer,
    top_skeleton,
    near_src,
    near_count,
    far_src,
    far_count,
    top_src,
    top_count,
):
    rhs, width = charges.shape
    leaves, rank, points = leaf_basis.shape
    near = near_src.shape[1]
    branches = lax.axis_size("br")
    height = table_height(leaves, near)
    shape = jax.ShapeDtypeStruct
    like = lambda x: shape(x.shape, x.dtype)
    cost = lambda us: pl.CostEstimate(
        flops=int(us * 1e6), bytes_accessed=int(us * 3e6), transcendentals=0
    )
    swap = [(0, 1), (1, 0)]
    order = order.reshape(leaves, points)
    partner = lax.ppermute(charges, "sub", swap)
    fetched = [
        charges, order, coords, near_src, near_count.reshape(1, leaves),
        leaf_basis, leaf_transfer, branch_transfer, upper_transfer, top_skeleton,
        far_src.T, far_count, top_src.T, top_count,
    ]
    (
        own, order, near_src, near_count,
        leaf_basis, leaf_transfer, branch_transfer, upper_transfer, top_skeleton,
        far_src, far_count, top_src, top_count,
        feats, tall,
    ) = pl.pallas_call(
        prepare,
        out_shape=tuple(like(x) for i, x in enumerate(fetched) if i != 2)
        + (shape((FEAT, width), bf16), shape((3 * FEAT, width), bf16)),
        in_specs=[HBM] * len(fetched),
        out_specs=(VMEM,) * 9 + (SMEM,) * 4 + (VMEM, VMEM),
        scratch_shapes=[
            pltpu.VMEM(coords.shape, f32),
            pltpu.VMEM((FEAT, width), f32),
            pltpu.VMEM((3 * FEAT, width), f32),
            pltpu.SemaphoreType.DMA((len(fetched),)),
        ],
        compiler_params=params,
        cost_estimate=cost(2),
        name="prepare",
    )(*(pltpu.with_memory_space_constraint(x, pltpu.HBM) for x in fetched))
    chunks = 2 * rhs * width // CHUNK
    pack, up = pl.pallas_call(
        upward,
        out_shape=(
            shape((rhs + FEAT + rhs // 2, width), bf16),
            shape((rhs + rhs // 2, 2 * rank), f32),
        ),
        in_specs=[VMEM] * 8,
        out_specs=(VMEM, VMEM),
        scratch_shapes=[
            pltpu.VMEM((chunks, CHUNK), bf16),
            pltpu.VMEM((rhs, leaves * rank), bf16),
            *[pltpu.VMEM((CHUNK, CHUNK), bf16)] * 2,
            *[pltpu.VMEM((chunks, CHUNK), f32)] * 2,
            *[pltpu.VMEM((rhs * CHUNK // points, 2 * rank), f32)] * 2,
        ],
        compiler_params=params,
        cost_estimate=cost(6),
        name="upward",
    )(
        own, partner, order, feats,
        leaf_basis, leaf_transfer, branch_transfer, upper_transfer,
    )
    near_tab, far_tab, target = pl.pallas_call(
        turn,
        out_shape=(shape((height, WIDE), jnp.int32),) * 2 + (shape((width, 3 * FEAT), bf16),),
        in_specs=[VMEM] * 3,
        out_specs=(SMEM, SMEM, VMEM),
        scratch_shapes=[pltpu.VMEM((2, height, WIDE), jnp.int32), pltpu.SemaphoreType.DMA((2,))],
        compiler_params=params,
        cost_estimate=cost(2),
        name="turn",
    )(near_src, near_count, tall)
    exchange = lambda x, bit: lax.ppermute(x, "br", [(i, i ^ (1 << bit)) for i in range(branches)])
    other, near_tab, far_tab, target = lax.optimization_barrier(
        (lax.ppermute(up, "sub", swap), near_tab, far_tab, target)
    )
    mine = up + other
    theirs = exchange(mine, 0)
    mine, top_skeleton = lax.optimization_barrier((mine, top_skeleton))
    tops = pl.pallas_call(
        top_kernels,
        out_shape=shape((3, rank, top_src.shape[0] * rank), f32),
        in_specs=[SMEM, VMEM],
        out_specs=VMEM,
        scratch_shapes=[pltpu.VMEM((8, 128), f32)],
        compiler_params=params,
        cost_estimate=cost(1),
        name="top_kernels",
    )(top_src, top_skeleton)
    held, tops = lax.optimization_barrier((pack, tops))
    between = [(2 * j + 1, 2 * j + 2) for j in range(branches - 1)]
    outer = lax.ppermute(held, ("br", "sub"), between + [(b, a) for a, b in between])
    mine, theirs, held = lax.optimization_barrier((mine, theirs, held))
    inner = lax.ppermute(held, "sub", swap)
    pipeline = [pltpu.VMEM((points, 2 * Q * points), f32)] * UNROLL + [
        pltpu.VMEM((points, 2 * Q * points), bf16)
    ] * UNROLL

    def local():
        return pl.pallas_call(
            near_local,
            out_shape=shape((rhs, width), f32),
            in_specs=[SMEM, VMEM, VMEM],
            out_specs=VMEM,
            scratch_shapes=[
                pltpu.VMEM((FEAT, width + points), bf16),
                pltpu.VMEM((rhs, width + points), bf16),
            ]
            + pipeline,
            compiler_params=params,
            cost_estimate=cost(6),
            name="near_local",
        )(near_tab, held, target)

    for bit in range(1, branches.bit_length() - 1):
        mine = jnp.concatenate([mine, theirs], axis=0)
        theirs = exchange(mine, bit)
        if bit == branches.bit_length() - 3:
            theirs, start = lax.optimization_barrier((theirs, local()))
    both, field = pl.pallas_call(
        near_remote,
        out_shape=(shape((rhs, width), f32), shape((rhs, leaves * rank), f32)),
        in_specs=[SMEM] * 3 + [VMEM] * 5,
        out_specs=(VMEM, VMEM),
        scratch_shapes=[
            pltpu.VMEM((FEAT, 3 * width + points), bf16),
            pltpu.VMEM((rhs, 3 * width + points), bf16),
            pltpu.VMEM((rhs, 3 * width + points), bf16),
        ]
        + pipeline,
        compiler_params=params,
        cost_estimate=cost(14),
        name="near_remote",
    )(far_tab, far_src, far_count, outer, inner, held, target, start)
    return pl.pallas_call(
        downward,
        out_shape=shape((rhs, width), f32),
        in_specs=[SMEM, SMEM] + [VMEM] * 9,
        out_specs=VMEM,
        scratch_shapes=[
            pltpu.VMEM((branches * up.shape[0], 2 * rank), f32),
            pltpu.VMEM((2 * rhs, leaves * rank), bf16),
        ],
        compiler_params=params,
        cost_estimate=cost(4),
        name="downward",
    )(
        top_src, top_count, mine, theirs, tops, both, field,
        leaf_basis, leaf_transfer, branch_transfer, upper_transfer,
    )


def solution(mesh):
    return jax.shard_map(
        shards,
        mesh=mesh,
        in_specs=(
            P(None, ("grp", "br", "sub")),
            P(("grp", "br", "sub")),
            P(None, ("grp", "br", "sub")),
            P(("grp", "br", "sub"), None, None),
            P(("grp", "br", "sub"), None, None),
            P(("grp", "br"), None, None),
            P("grp", None, None),
            P(None, "grp"),
            P(("grp", "br", "sub"), None),
            P(("grp", "br", "sub")),
            P(("grp", "br", "sub"), None),
            P(("grp", "br", "sub")),
            P("grp", None),
            P("grp"),
        ),
        out_specs=P(None, ("grp", "br", "sub")),
        check_vma=False,
    )
```

```python
import jax
import jax.numpy as jnp
from jax import lax
from jax.experimental import pallas as pl
from jax.experimental.pallas import tpu as pltpu
from jax.sharding import PartitionSpec as P

scale = 1.7320508075688772 / 0.25
f32 = jnp.float32
bf16 = jnp.bfloat16
HIGHEST = lax.Precision.HIGHEST
NT = (((1,), (1,)), ((), ()))
Q = 4
UNROLL = 3
WIDE = 32
FEAT = 16
CHUNK = 256
VMEM = pl.BlockSpec(memory_space=pltpu.VMEM)
SMEM = pl.BlockSpec(memory_space=pltpu.SMEM)
HBM = pl.BlockSpec(memory_space=pltpu.HBM)
params = pltpu.CompilerParams(vmem_limit_bytes=28 << 20)


def profile_of(squared):
    squared = jnp.maximum(squared, 1e-12)
    scaled = squared * lax.rsqrt(squared)
    return (1.0 + scaled) * jnp.exp(-scaled)


def split(x):
    first = x.astype(bf16).astype(f32)
    rest = x - first
    second = rest.astype(bf16).astype(f32)
    return first, second, (rest - second).astype(bf16).astype(f32)


def permute(rows, order, store, extra, hots, picks, rhs):
    per = CHUNK // order.shape[1]
    groups = rows.shape[0] // rhs
    blocks = order.shape[0] // per
    cuts = 4

    def within(c):
        return jnp.clip(c, 0, blocks - 1)

    def where_from(c):
        return jnp.concatenate([order[pl.ds(within(c) * per + i, 1), :] for i in range(per)], axis=1)

    def step(i, state):
        for u in range(2):
            c = 2 * i + u
            low = where_from(c) & (CHUNK - 1)
            high = where_from(c - 2) >> (CHUNK.bit_length() - 1)
            at = pl.ds(pl.multiple_of(within(c - 2) * CHUNK, CHUNK), CHUNK)
            found = jnp.zeros((rhs, CHUNK), f32)
            tall = rows.shape[0] // cuts
            for k in range(cuts):
                part = slice(k * tall, (k + 1) * tall)
                picks[u][part, :] = jnp.dot(rows[part, :], hots[1 - u][...], preferred_element_type=f32)
                for h in range(k * groups // cuts, (k + 1) * groups // cuts):
                    found = jnp.where(high == h, picks[1 - u][h * rhs : (h + 1) * rhs, :], found)
                lines = CHUNK // cuts
                line = lax.broadcasted_iota(jnp.int32, (lines, CHUNK), 0) + k * lines
                hots[u][k * lines : (k + 1) * lines, :] = jnp.where(line == low, 1.0, 0.0).astype(bf16)
            store(at, found.astype(bf16))
            extra(c, u, within)
        return state

    lax.fori_loop(0, (blocks + 5) // 2, step, 0)


def make_lists(flags, source, nones, height):
    leaves, near = source.shape
    before = lax.broadcasted_iota(jnp.int32, (near, near), 0) < lax.broadcasted_iota(jnp.int32, (near, near), 1)
    before = jnp.where(before, 1.0, 0.0).astype(bf16)
    above = lax.broadcasted_iota(jnp.int32, (leaves, leaves), 1) < lax.broadcasted_iota(jnp.int32, (leaves, leaves), 0)
    above = jnp.where(above, 1.0, 0.0).astype(bf16)
    packed = jnp.full((leaves, near), -1, jnp.int32)
    pairs = []
    for k, flag in enumerate(flags):
        ones = jnp.where(flag, 1.0, 0.0)
        number = jnp.sum(ones, axis=1, keepdims=True).astype(jnp.int32)
        even = (number + (number & 1)).astype(f32)
        place = jnp.dot(ones.astype(bf16), before, preferred_element_type=f32) + jnp.dot(
            above, jnp.broadcast_to(even, (leaves, near)).astype(bf16), preferred_element_type=f32
        )
        place = place.astype(jnp.int32) + (4 * Q + k * height * WIDE)
        packed = jnp.where(flag, place * 128 + source + 1, packed)
        pairs.append((jnp.sum(even, axis=0, keepdims=True) * 0.5).astype(jnp.int32))
    wide = max(2 * height, 2 * WIDE)
    lane = lax.broadcasted_iota(jnp.int32, (leaves, wide), 1)
    leaf = lax.broadcasted_iota(jnp.int32, (leaves, wide), 0)
    left, right = [], []
    for j in range(near):
        entry = jnp.broadcast_to(packed[:, j : j + 1], (leaves, wide))
        place = entry >> 7
        left.append(jnp.where(lane == place >> (WIDE.bit_length() - 1), 1.0, 0.0).astype(bf16))
        value = jnp.where(lane < WIDE, leaf, entry & 127)
        right.append(jnp.where(((lane ^ place) & (WIDE - 1)) == 0, value, 0).astype(f32).astype(bf16))
    out = lax.dot_general(
        jnp.concatenate(left, axis=0),
        jnp.concatenate(right, axis=0),
        (((0,), (0,)), ((), ())),
        preferred_element_type=f32,
    ).astype(jnp.int32)
    shape = (height, WIDE)
    last = lax.broadcasted_iota(jnp.int32, shape, 0) * WIDE + lax.broadcasted_iota(jnp.int32, shape, 1)
    lists = []
    for k, none in enumerate(nones):
        lines = slice(k * height, (k + 1) * height)
        found = out[lines, WIDE : 2 * WIDE]
        code = out[lines, :WIDE] * 256 + 2 * jnp.where(found == 0, none, found - 1)
        lists.append(jnp.where(last == height * WIDE - 1, pairs[k], code))
    return lists


def prepare(*refs):
    fetched = 14
    sources = refs[:fetched]
    charges, order, near_src, near_count = refs[fetched : fetched + 4]
    kept = refs[fetched + 4 : fetched + 13]
    feats, tall = refs[fetched + 13 : fetched + 15]
    coords, wide, high, sems = refs[fetched + 15 :]
    copies = [
        pltpu.make_async_copy(source, dest, sems.at[i])
        for i, (source, dest) in enumerate(
            zip(sources, (charges, order, coords, near_src, near_count) + tuple(kept))
        )
    ]
    for copy in copies:
        copy.start()
    wide[...] = jnp.zeros_like(wide)
    high[...] = jnp.zeros_like(high)
    copies[2].wait()
    place = (coords[...] - 0.5) * scale
    r1, r2, r3 = split(place)
    n1, n2, n3 = split(
        place[0:1] * place[0:1] + place[1:2] * place[1:2] + place[2:3] * place[2:3]
    )
    one = jnp.ones_like(n1)
    wide[0:3, :] = -2.0 * r1
    wide[3:6, :] = -2.0 * r2
    wide[6:9, :] = -2.0 * r3
    wide[9:10, :] = n1
    wide[10:11, :] = n2
    wide[11:12, :] = n3
    wide[12:13, :] = one
    feats[...] = wide[...].astype(bf16)
    for i in range(3):
        high[3 * i : 3 * i + 3, :] = r1
        high[9 + i : 10 + i, :] = one
    high[12:13, :] = n1
    high[16:19, :] = r2
    high[19:22, :] = r2
    high[28:29, :] = n2
    high[32:35, :] = r3
    high[44:45, :] = n3
    tall[...] = high[...].astype(bf16)
    for i in (0, 1, *range(3, fetched)):
        copies[i].wait()


def turn(near_src, near_count, tall, near_tab, far_tab, target, coded, sems):
    leaves, near = near_src.shape
    square = (leaves, leaves)
    diagonal = lax.broadcasted_iota(jnp.int32, square, 0) == lax.broadcasted_iota(jnp.int32, square, 1)
    live = jnp.sum(jnp.where(diagonal, near_count[...], 0), axis=1, keepdims=True)
    valid = lax.broadcasted_iota(jnp.int32, (leaves, near), 1) < live
    offset = near_src[...] - lax.axis_index(("br", "sub")) * leaves
    here = (offset >= 0) & (offset < leaves)
    height = coded.shape[1]
    flags = (valid & here, valid & jnp.logical_not(here))
    source = jnp.where(here, offset, offset + leaves)
    coded[0], coded[1] = make_lists(flags, source, (leaves, 3 * leaves), height)
    copies = [pltpu.make_async_copy(coded.at[i], tab, sems.at[i]) for i, tab in enumerate((near_tab, far_tab))]
    for copy in copies:
        copy.start()
    square = (128, 128)
    one = jnp.where(
        lax.broadcasted_iota(jnp.int32, square, 0) == lax.broadcasted_iota(jnp.int32, square, 1), 1.0, 0.0
    ).astype(bf16)
    for at in range(0, tall.shape[1], 128):
        target[at : at + 128, :] = lax.dot_general(
            one, tall[:, at : at + 128], NT, preferred_element_type=f32
        ).astype(bf16)
    for copy in copies:
        copy.wait()


def node_places(skeleton, node, rank):
    both = skeleton[:, pl.ds(pl.multiple_of((node >> 1) * (2 * rank), 2 * rank), 2 * rank)]
    return jnp.where((node & 1) == 1, both[:, rank:], both[:, :rank])


def top_kernels(top_src, skeleton, tops, places):
    fan = top_src.shape[0]
    rank = tops.shape[1]
    places[...] = jnp.zeros_like(places)
    offset = 0
    for level in range(3):
        nodes = lax.axis_size("br") >> level
        row = offset + (lax.axis_index("br") >> level)
        places[0:3, 0:rank] = node_places(skeleton, row, rank)
        own = places[...].T
        kernels = []
        for j in range(fan):
            there = node_places(skeleton, offset + jnp.minimum(top_src[j, row], nodes - 1), rank)
            squared = None
            for d in range(3):
                gap = (there[d : d + 1, :] - own[0:rank, d : d + 1]) * scale
                squared = gap * gap if squared is None else squared + gap * gap
            kernels.append(profile_of(squared))
        tops[level] = jnp.concatenate(kernels, axis=1)
        offset += nodes


def table_height(leaves, near):
    need = 4 * Q + leaves * (near + near % 2) + 2 * Q * (UNROLL + 4) + 1
    return -(-need // (8 * WIDE)) * 8


def upward(
    charges, partner, order, feats, basis, transfer, branch_transfer, upper_transfer,
    pack, up, rows, packed, *pipes,
):
    leaves, points = order.shape
    rhs = charges.shape[0]
    rank = basis.shape[1]
    blocks = charges.shape[1] // CHUNK
    own = lax.axis_index("sub") * blocks
    for h in range(blocks):
        for at, ref in ((own + h, charges), (blocks - own + h, partner)):
            rows[pl.ds(pl.multiple_of(at * rhs, rhs), rhs), :] = ref[:, h * CHUNK : (h + 1) * CHUNK]
    pack[rhs : rhs + FEAT, :] = feats[...]
    per = CHUNK // points
    early = lax.broadcasted_iota(jnp.int32, (rhs, 2 * rank), 1) < rank
    hots, picks, raw = pipes[:2], pipes[2:4], pipes[4:]

    def columns(leaf):
        return pl.ds(pl.multiple_of(leaf * points, points), points)

    def extra(c, u, within):
        for pair in range(per // 2):
            lines = slice(2 * rhs * pair, 2 * rhs * (pair + 1))
            leaf = within(c - 4) * per + 2 * pair
            both = raw[1 - u][lines, :]
            coef = jnp.where(early, both[:rhs], both[rhs:])
            packed[:, columns(leaf >> 1)] = coef.astype(bf16)
            leaf = within(c - 3) * per + 2 * pair
            raw[u][lines, :] = lax.dot_general(
                jnp.concatenate([pack[0:rhs, columns(leaf)], pack[0:rhs, columns(leaf + 1)]], axis=0),
                basis[pl.ds(leaf, 2)].reshape(2 * rank, points),
                NT,
                preferred_element_type=f32,
            )

    def store(at, found):
        pack[0:rhs, at] = found

    permute(rows, order, store, extra, hots, picks, rhs)
    half = rhs // 2
    pack[rhs + FEAT :, : leaves * rank] = packed[:half, :]
    pack[rhs + FEAT :, leaves * rank :] = packed[half:, :]
    total = jnp.dot(packed[...], transfer[...].reshape(leaves * rank, rank), preferred_element_type=f32)
    lifted = jnp.dot(total, branch_transfer[0].astype(f32), precision=HIGHEST)
    parent = lax.axis_index("br") // 2
    second = jnp.dot(lifted, upper_transfer[parent].astype(f32), precision=HIGHEST)
    up[0:rhs, 0:rank] = total
    up[0:rhs, rank : 2 * rank] = lifted
    up[rhs : rhs + half, 0:rank] = second[:half]
    up[rhs : rhs + half, rank : 2 * rank] = second[half:]


def near_items(tab, target, sources, values, out, distances, kernels, points):
    total = (tab[tab.shape[0] - 1, WIDE - 1] + Q - 1) // Q
    for distance, kernel in zip(distances, kernels):
        distance[...] = jnp.full(distance.shape, 1e6, f32)
        kernel[...] = jnp.zeros_like(kernel)

    def columns(leaf):
        return pl.ds(pl.multiple_of(leaf * points, points), points)

    def decode(item, q):
        at = (item * Q + q) * 2
        high, low = at >> (WIDE.bit_length() - 1), at & (WIDE - 1)
        one, two = tab[high, low], tab[high, low + 1]
        return columns(one >> 8), columns((one >> 1) & 127), columns((two >> 1) & 127)

    def step(i, _):
        for u in range(UNROLL):
            item = i * UNROLL + u
            behind, last = (u - 1) % UNROLL, (u - 2) % UNROLL
            for q in range(Q):
                part = slice(2 * q * points, 2 * (q + 1) * points)
                leaf, one, two = decode(item, q)
                value = lax.dot_general(
                    jnp.concatenate([values[:, one], values[:, two]], axis=1),
                    kernels[last][:, part],
                    NT,
                    preferred_element_type=f32,
                )
                kernels[behind][:, part] = profile_of(distances[behind][:, part]).astype(bf16)
                target_leaf, one, two = decode(item + 2, q)
                pair = jnp.concatenate([sources[:, one], sources[:, two]], axis=1)
                distances[u][:, part] = jnp.dot(
                    target[target_leaf, :],
                    jnp.concatenate([pair, pair, pair], axis=0),
                    preferred_element_type=f32,
                )
                out[:, leaf] += value
        return 0

    lax.fori_loop(0, (total + 2 + UNROLL - 1) // UNROLL, step, 0)


def near_local(tab, pack, target, out, sources, values, *scratch):
    rhs, width = out.shape
    points = sources.shape[1] - width
    sources[:, :width] = pack[rhs : rhs + FEAT, :]
    sources[:, width:] = jnp.zeros_like(sources[:, width:])
    values[:, :width] = pack[0:rhs, :]
    values[:, width:] = jnp.zeros_like(values[:, width:])
    out[...] = jnp.zeros_like(out)
    near_items(tab, target, sources, values, out, scratch[:UNROLL], scratch[UNROLL:], points)


def near_remote(
    tab, far_src, far_count, outer, inner, pack, target, start, out, field,
    sources, values, coefs, *scratch
):
    rhs, width = out.shape
    far, leaves = far_src.shape
    points = width // leaves
    rank = field.shape[1] // leaves
    none = 3 * leaves
    side = 2 * lax.axis_index("sub")
    for at, ref in ((side * width, outer), ((2 - side) * width, inner), (width, pack)):
        to = pl.ds(pl.multiple_of(at, width), width)
        sources[:, to] = ref[rhs : rhs + FEAT, :]
        values[:, to] = ref[0:rhs, :]
    early_values = lax.broadcasted_iota(jnp.int32, (rhs, points), 1) < rank
    half = leaves * rank
    for window, ref in ((side, outer), (2 - side, inner), (1, pack)):
        for i in range(leaves // 2):
            at = i * points
            block = jnp.concatenate(
                [
                    ref[rhs + FEAT :, at : at + points].astype(f32),
                    ref[rhs + FEAT :, half + at : half + at + points].astype(f32),
                ],
                axis=0,
            )
            turned = pltpu.roll(block, rank, 1)
            for k, twice in enumerate(((block, turned), (turned, block))):
                to = pl.ds(pl.multiple_of((window * leaves + 2 * i + k) * points, points), points)
                coefs[:, to] = jnp.where(early_values, *twice).astype(bf16)
    for ref in (sources, values, coefs):
        ref[:, none * points :] = jnp.zeros_like(ref[:, none * points :])
    out[...] = start[...]
    distances, kernels = scratch[:UNROLL], scratch[UNROLL:]
    near_items(tab, target, sources, values, out, distances, kernels, points)
    early = lax.broadcasted_iota(jnp.int32, (FEAT, points), 1) < rank
    base = (lax.axis_index(("br", "sub")) - 1) * leaves

    def columns(leaf):
        return pl.ds(pl.multiple_of(leaf * points, points), points)

    def picked(leaf, j):
        if j >= far:
            return columns(none)
        return columns(jnp.where(j < far_count[leaf], far_src[j, leaf] - base, none))

    items = leaves // 2
    groups = (far + 1) // 2
    wide = groups * points

    def far_step(i, _):
        for u in range(2 * UNROLL):
            item = 2 * i * UNROLL + u
            behind, last = (u - 1) % UNROLL, (u - 2) % UNROLL
            done = jnp.clip(item - 2, 0, items - 1)
            ahead = jnp.minimum(item, items - 1)
            pairs = [[], []]
            for k in range(2):
                for g in range(groups):
                    one, two = picked(2 * done + k, 2 * g), picked(2 * done + k, 2 * g + 1)
                    pairs[k].append(jnp.where(early_values, coefs[:, one], coefs[:, two]))
            total = lax.dot_general(
                jnp.concatenate([jnp.concatenate(pair, axis=1) for pair in pairs], axis=0),
                kernels[last][:, :wide],
                NT,
                preferred_element_type=f32,
            )
            for k in range(2):
                lines = slice(k * rank, (k + 1) * rank)
                kernels[behind][lines, :wide] = profile_of(distances[behind][lines, :wide]).astype(bf16)
                leaf = 2 * ahead + k
                places = []
                for g in range(groups):
                    one, two = picked(leaf, 2 * g), picked(leaf, 2 * g + 1)
                    turned = pltpu.roll(sources[:, two].astype(f32), rank, 1)
                    places.append(jnp.where(early, sources[:, one].astype(f32), turned).astype(bf16))
                places = jnp.concatenate(places, axis=1)
                distances[u % UNROLL][lines, :wide] = jnp.dot(
                    target[pl.ds(pl.multiple_of(leaf * points, points), rank), :],
                    jnp.concatenate([places] * 3, axis=0),
                    preferred_element_type=f32,
                )
            field[:, columns(done)] = jnp.where(early_values, total[:rhs], total[rhs:])
        return 0

    lax.fori_loop(0, (items + 2 + 2 * UNROLL - 1) // (2 * UNROLL), far_step, 0)


def downward(
    top_src, top_count, mine, theirs, tops, near, field, basis, transfer, branch_transfer, upper_transfer, out, every, halves
):
    rhs = near.shape[0]
    leaves, rank, points = basis.shape
    branches = lax.axis_size("br")
    branch = lax.axis_index("br")
    depth = every.shape[0] // branches
    half = rhs // 2
    fan = top_src.shape[0]
    every[0 : mine.shape[0], :] = mine[...]
    every[mine.shape[0] :, :] = theirs[...]

    def coefficients(level, node):
        total = None
        for d in range(1 << level):
            at = pl.multiple_of((((node << level) + d) ^ branch) * depth, 8)
            if level < 2:
                block = every[pl.ds(at, rhs), :]
            else:
                block = every[pl.ds(at + rhs, half), :]
            total = block if total is None else total + block
        if level == 0:
            return total[:, :rank]
        if level == 1:
            return total[:, rank:]
        return jnp.concatenate([total[:, :rank], total[:, rank:]], axis=0)

    offset = 0
    fields = []
    for level in range(3):
        node = branch >> level
        row = offset + node
        coefs = []
        for j in range(fan):
            source = jnp.minimum(top_src[j, row], (branches >> level) - 1)
            coefs.append(jnp.where(j < top_count[row], coefficients(level, source), 0.0))
        fields.append(
            lax.dot_general(
                jnp.concatenate(coefs, axis=1),
                tops[level],
                NT,
                precision=HIGHEST,
                preferred_element_type=f32,
            )
        )
        offset += branches >> level
    down_one = fields[1] + lax.dot_general(
        fields[2], upper_transfer[branch >> 1].astype(f32), NT, precision=HIGHEST, preferred_element_type=f32
    )
    down_zero = fields[0] + lax.dot_general(
        down_one, branch_transfer[0].astype(f32), NT, precision=HIGHEST, preferred_element_type=f32
    )
    down_zero = down_zero.astype(bf16)
    down = field[...] + lax.dot_general(
        down_zero, transfer[...].reshape(leaves * rank, rank), NT, preferred_element_type=f32
    )
    early = (lax.broadcasted_iota(jnp.int32, down.shape, 1) & (2 * rank - 1)) < rank
    halves[0:rhs, :] = jnp.where(early, down, 0.0).astype(bf16)
    halves[rhs:, :] = jnp.where(early, 0.0, down).astype(bf16)
    for i in range(leaves // 2):
        at = 2 * i * rank
        value = jnp.dot(
            halves[:, at : at + 2 * rank],
            basis[2 * i : 2 * i + 2].reshape(2 * rank, points),
            preferred_element_type=f32,
        )
        for k in range(2):
            col = (2 * i + k) * points
            out[:, col : col + points] = near[:, col : col + points] + value[k * rhs : (k + 1) * rhs]


def shards(
    charges,
    order,
    coords,
    leaf_basis,
    leaf_transfer,
    branch_transfer,
    upper_transfer,
    top_skeleton,
    near_src,
    near_count,
    far_src,
    far_count,
    top_src,
    top_count,
):
    rhs, width = charges.shape
    leaves, rank, points = leaf_basis.shape
    near = near_src.shape[1]
    branches = lax.axis_size("br")
    height = table_height(leaves, near)
    shape = jax.ShapeDtypeStruct
    like = lambda x: shape(x.shape, x.dtype)
    cost = lambda us: pl.CostEstimate(
        flops=int(us * 1e6), bytes_accessed=int(us * 3e6), transcendentals=0
    )
    swap = [(0, 1), (1, 0)]
    order = order.reshape(leaves, points)
    partner = lax.ppermute(charges, "sub", swap)
    fetched = [
        charges, order, coords, near_src, near_count.reshape(1, leaves),
        leaf_basis, leaf_transfer, branch_transfer, upper_transfer, top_skeleton,
        far_src.T, far_count, top_src.T, top_count,
    ]
    (
        own, order, near_src, near_count,
        leaf_basis, leaf_transfer, branch_transfer, upper_transfer, top_skeleton,
        far_src, far_count, top_src, top_count,
        feats, tall,
    ) = pl.pallas_call(
        prepare,
        out_shape=tuple(like(x) for i, x in enumerate(fetched) if i != 2)
        + (shape((FEAT, width), bf16), shape((3 * FEAT, width), bf16)),
        in_specs=[HBM] * len(fetched),
        out_specs=(VMEM,) * 9 + (SMEM,) * 4 + (VMEM, VMEM),
        scratch_shapes=[
            pltpu.VMEM(coords.shape, f32),
            pltpu.VMEM((FEAT, width), f32),
            pltpu.VMEM((3 * FEAT, width), f32),
            pltpu.SemaphoreType.DMA((len(fetched),)),
        ],
        compiler_params=params,
        cost_estimate=cost(2),
        name="prepare",
    )(*(pltpu.with_memory_space_constraint(x, pltpu.HBM) for x in fetched))
    chunks = 2 * rhs * width // CHUNK
    pack, up = pl.pallas_call(
        upward,
        out_shape=(
            shape((rhs + FEAT + rhs // 2, width), bf16),
            shape((rhs + rhs // 2, 2 * rank), f32),
        ),
        in_specs=[VMEM] * 8,
        out_specs=(VMEM, VMEM),
        scratch_shapes=[
            pltpu.VMEM((chunks, CHUNK), bf16),
            pltpu.VMEM((rhs, leaves * rank), bf16),
            *[pltpu.VMEM((CHUNK, CHUNK), bf16)] * 2,
            *[pltpu.VMEM((chunks, CHUNK), f32)] * 2,
            *[pltpu.VMEM((rhs * CHUNK // points, 2 * rank), f32)] * 2,
        ],
        compiler_params=params,
        cost_estimate=cost(6),
        name="upward",
    )(
        own, partner, order, feats,
        leaf_basis, leaf_transfer, branch_transfer, upper_transfer,
    )
    near_tab, far_tab, target = pl.pallas_call(
        turn,
        out_shape=(shape((height, WIDE), jnp.int32),) * 2 + (shape((width, 3 * FEAT), bf16),),
        in_specs=[VMEM] * 3,
        out_specs=(SMEM, SMEM, VMEM),
        scratch_shapes=[pltpu.VMEM((2, height, WIDE), jnp.int32), pltpu.SemaphoreType.DMA((2,))],
        compiler_params=params,
        cost_estimate=cost(2),
        name="turn",
    )(near_src, near_count, tall)
    exchange = lambda x, bit: lax.ppermute(x, "br", [(i, i ^ (1 << bit)) for i in range(branches)])
    other, near_tab, far_tab, target = lax.optimization_barrier(
        (lax.ppermute(up, "sub", swap), near_tab, far_tab, target)
    )
    mine = up + other
    theirs = exchange(mine, 0)
    mine, top_skeleton = lax.optimization_barrier((mine, top_skeleton))
    tops = pl.pallas_call(
        top_kernels,
        out_shape=shape((3, rank, top_src.shape[0] * rank), f32),
        in_specs=[SMEM, VMEM],
        out_specs=VMEM,
        scratch_shapes=[pltpu.VMEM((8, 128), f32)],
        compiler_params=params,
        cost_estimate=cost(1),
        name="top_kernels",
    )(top_src, top_skeleton)
    held, tops = lax.optimization_barrier((pack, tops))
    between = [(2 * j + 1, 2 * j + 2) for j in range(branches - 1)]
    outer = lax.ppermute(held, ("br", "sub"), between + [(b, a) for a, b in between])
    mine, theirs, held = lax.optimization_barrier((mine, theirs, held))
    inner = lax.ppermute(held, "sub", swap)
    pipeline = [pltpu.VMEM((points, 2 * Q * points), f32)] * UNROLL + [
        pltpu.VMEM((points, 2 * Q * points), bf16)
    ] * UNROLL

    def local():
        return pl.pallas_call(
            near_local,
            out_shape=shape((rhs, width), f32),
            in_specs=[SMEM, VMEM, VMEM],
            out_specs=VMEM,
            scratch_shapes=[
                pltpu.VMEM((FEAT, width + points), bf16),
                pltpu.VMEM((rhs, width + points), bf16),
            ]
            + pipeline,
            compiler_params=params,
            cost_estimate=cost(6),
            name="near_local",
        )(near_tab, held, target)

    for bit in range(1, branches.bit_length() - 1):
        mine = jnp.concatenate([mine, theirs], axis=0)
        theirs = exchange(mine, bit)
        if bit == branches.bit_length() - 3:
            theirs, start = lax.optimization_barrier((theirs, local()))
    both, field = pl.pallas_call(
        near_remote,
        out_shape=(shape((rhs, width), f32), shape((rhs, leaves * rank), f32)),
        in_specs=[SMEM] * 3 + [VMEM] * 5,
        out_specs=(VMEM, VMEM),
        scratch_shapes=[
            pltpu.VMEM((FEAT, 3 * width + points), bf16),
            pltpu.VMEM((rhs, 3 * width + points), bf16),
            pltpu.VMEM((rhs, 3 * width + points), bf16),
        ]
        + pipeline,
        compiler_params=params,
        cost_estimate=cost(14),
        name="near_remote",
    )(far_tab, far_src, far_count, outer, inner, held, target, start)
    return pl.pallas_call(
        downward,
        out_shape=shape((rhs, width), f32),
        in_specs=[SMEM, SMEM] + [VMEM] * 9,
        out_specs=VMEM,
        scratch_shapes=[
            pltpu.VMEM((branches * up.shape[0], 2 * rank), f32),
            pltpu.VMEM((2 * rhs, leaves * rank), bf16),
        ],
        compiler_params=params,
        cost_estimate=cost(4),
        name="downward",
    )(
        top_src, top_count, mine, theirs, tops, both, field,
        leaf_basis, leaf_transfer, branch_transfer, upper_transfer,
    )


def solution(mesh):
    return jax.shard_map(
        shards,
        mesh=mesh,
        in_specs=(
            P(None, ("grp", "br", "sub")),
            P(("grp", "br", "sub")),
            P(None, ("grp", "br", "sub")),
            P(("grp", "br", "sub"), None, None),
            P(("grp", "br", "sub"), None, None),
            P(("grp", "br"), None, None),
            P("grp", None, None),
            P(None, "grp"),
            P(("grp", "br", "sub"), None),
            P(("grp", "br", "sub")),
            P(("grp", "br", "sub"), None),
            P(("grp", "br", "sub")),
            P("grp", None),
            P("grp"),
        ),
        out_specs=P(None, ("grp", "br", "sub")),
        check_vma=False,
    )
```
